256 devices in a mesh: dp: 4 (over z_lo, core), ctx: 64 (over x, y, z_hi).
Axes of the slice: x: 4, y: 4, z: 8 (z_hi: 4, z_lo: 2; z = z_hi * 2 + z_lo), core: 2. Of those that a mesh axis runs over, the one named last changes fastest.
Arguments:
- queries: bfloat16 [4, 8192, 1024], P('dp', 'ctx'), may hold values from -12 to 12
- keys: bfloat16 [4, 8192, 1024], P('dp', 'ctx'), may hold values from -4 to 4
- values: bfloat16 [4, 8192, 1024], P('dp', 'ctx'), may hold values from -18 to 18
- out_grad: bfloat16 [4, 8192, 1024], P('dp', 'ctx'), may hold values from -6 to 6
- w_out: bfloat16 [1024, 1024], replicated, may hold values from -0.1875 to 0.1875
Outputs:
- layer_out: bfloat16 [4, 8192, 1024], P('dp', 'ctx')
- query_grad: bfloat16 [4, 8192, 1024], P('dp', 'ctx')
- key_grad: bfloat16 [4, 8192, 1024], P('dp', 'ctx')
- value_grad: bfloat16 [4, 8192, 1024], P('dp', 'ctx')
- weight_grad: float32 [1024, 1024], P('ctx')
The draws below stay inside these ranges and needn't reach their ends.
All inputs are finite; a program needn't handle non-finite values.
Results may differ from the reference program's by a relative error of at most 0.018.
Values may be sent and summed in bfloat16 or wider, within the bound.
No kernel may reach another device: no remote copies, remote signals or barrier semaphores. Data moves between devices by JAX's collectives and lax.ppermute only.
A program may use at most 64 MiB of HBM per device.

```python
import math
import jax
import jax.numpy as jnp
from jax import lax

D = 1024
DH = 64
STRIDE = 1024
SEQ = 8192
CLIPS = 4


def draw_queries(key, part):
    base_key = jax.random.fold_in(key, 5)
    drawn = jax.random.truncated_normal(base_key, -4.0, 4.0, (CLIPS, SEQ, D))
    return drawn.astype(jnp.bfloat16)


def draw_keys(key, part):
    base_key = jax.random.fold_in(key, 7)
    drawn = jax.random.truncated_normal(base_key, -4.0, 4.0, (CLIPS, SEQ, D))
    return drawn.astype(jnp.bfloat16)


def shard_levels(own_key, shape, shards, smallest, top_value):
    def one(dim, shards_of):
        draws = jax.random.uniform(jax.random.fold_in(jax.random.fold_in(own_key, 6), dim), (shards_of,), jnp.float32, smallest / len(shards), top_value / len(shards))
        return jnp.repeat(jnp.exp(draws), shape[dim] // shards_of).reshape((-1,) + (1,) * (len(shape) - dim - 1))

    gain = one(*shards[0])
    for cut in shards[1:]:
        gain = gain * one(*cut)
    return gain


def gaussian(stream_key, extent, width, bound, cuts=(), kind=jnp.bfloat16):
    factor_of = shard_levels(stream_key, extent, cuts, -0.22, 0.18) if cuts else 1.0
    values = jax.random.normal(stream_key, extent, jnp.float32) * width * factor_of
    return jnp.minimum(jnp.maximum(values, -bound), bound).astype(kind)


def setup_inputs(seed: int = 0) -> dict:
    arg_keys = jax.random.split(jax.random.key(seed), 6)
    queries = draw_queries(jax.random.fold_in(arg_keys[5], 71), 0)
    keys = draw_keys(jax.random.fold_in(arg_keys[5], 71), 0)
    values = gaussian(arg_keys[2], (CLIPS, SEQ, D), 3.0, 18.0, ((0, 4), (1, 64)))
    out_grad = gaussian(arg_keys[3], (CLIPS, SEQ, D), 1.0, 6.0, ((0, 4), (1, 64)))
    w_out = gaussian(arg_keys[4], (D, D), D ** -0.5, 0.1875)
    return dict(queries=queries, keys=keys, values=values, out_grad=out_grad, w_out=w_out)


def attend(q_part, k_part, v_part, g_part, allowed, score_scale):
    high = lax.Precision.HIGHEST
    f32 = jnp.float32
    scores = jnp.einsum('ntd,nsd->nts', q_part.astype(f32), k_part.astype(f32), precision=high) * score_scale
    masked = jnp.where(allowed, scores, -jnp.inf)
    row_max = lax.optimization_barrier(jnp.max(masked, axis=-1, keepdims=True))
    weights = jnp.exp(masked - row_max)
    probs_full = weights / lax.optimization_barrier(jnp.sum(weights, axis=-1, keepdims=True))
    probs_low = probs_full.astype(jnp.bfloat16)
    output = jnp.einsum('nts,nsd->ntd', probs_low.astype(f32), v_part.astype(f32), precision=high).astype(jnp.bfloat16)
    delta_sum = lax.optimization_barrier(jnp.sum(g_part.astype(f32) * output.astype(f32), axis=-1, keepdims=True))
    grad_dot = jnp.einsum('ntd,nsd->nts', g_part.astype(f32), v_part.astype(f32), precision=high)
    score_grad = (probs_full * (grad_dot - delta_sum)).astype(jnp.bfloat16)
    q_grad = (jnp.einsum('nts,nsd->ntd', score_grad.astype(f32), k_part.astype(f32), precision=high) * score_scale).astype(jnp.bfloat16)
    k_grad = jnp.einsum('nts,ntd->nsd', score_grad.astype(f32), q_part.astype(f32), precision=high) * score_scale
    v_grad = jnp.einsum('nts,ntd->nsd', probs_low.astype(f32), g_part.astype(f32), precision=high)
    return (output, q_grad, k_grad, v_grad)

def row_item(item, score_scale):
    q_one, k_one, v_one, g_one = item
    seq_len = q_one.shape[0]
    pad_rows = jnp.zeros((STRIDE, DH), k_one.dtype)
    k_pad = jnp.concatenate([pad_rows, k_one], axis=0)
    v_pad = jnp.concatenate([pad_rows, v_one], axis=0)
    block_count = seq_len // STRIDE
    row_iota = lax.broadcasted_iota(jnp.int32, (STRIDE, 2 * STRIDE), 0)
    col_iota = lax.broadcasted_iota(jnp.int32, (STRIDE, 2 * STRIDE), 1)

    def advance(carry, block_index):
        k_acc, v_acc = carry
        offset = block_index * STRIDE
        q_blk = lax.dynamic_slice_in_dim(q_one, offset, STRIDE, 0)
        g_blk = lax.dynamic_slice_in_dim(g_one, offset, STRIDE, 0)
        k_blk = lax.dynamic_slice_in_dim(k_pad, offset, 2 * STRIDE, 0)
        v_blk = lax.dynamic_slice_in_dim(v_pad, offset, 2 * STRIDE, 0)
        allowed = (col_iota > row_iota) & (col_iota <= row_iota + STRIDE) & (col_iota >= STRIDE - offset)
        output, q_grad, k_grad, v_grad = attend(q_blk[None], k_blk[None], v_blk[None], g_blk[None], allowed, score_scale)
        k_acc = lax.dynamic_update_slice_in_dim(k_acc, lax.dynamic_slice_in_dim(k_acc, offset, 2 * STRIDE, 0) + k_grad[0], offset, 0)
        v_acc = lax.dynamic_update_slice_in_dim(v_acc, lax.dynamic_slice_in_dim(v_acc, offset, 2 * STRIDE, 0) + v_grad[0], offset, 0)
        return ((k_acc, v_acc), (output[0], q_grad[0]))
    zero_acc = jnp.zeros((seq_len + STRIDE, DH), jnp.float32)
    (k_acc, v_acc), (out_rows, q_rows) = lax.scan(advance, (zero_acc, zero_acc), jnp.arange(block_count, dtype=jnp.int32))
    return (out_rows.reshape(seq_len, DH), q_rows.reshape(seq_len, DH), k_acc[STRIDE:].astype(jnp.bfloat16), v_acc[STRIDE:].astype(jnp.bfloat16))

def reference(queries, keys, values, out_grad, w_out):
    clip_count, seq_len, model_width = queries.shape
    half_width = model_width // 2
    head_count = half_width // DH
    score_scale = 1.0 / math.sqrt(DH)
    grad_flat = out_grad.reshape(clip_count * seq_len, model_width)
    attention_grad = jnp.dot(grad_flat, w_out.T, preferred_element_type=jnp.float32).astype(jnp.bfloat16).reshape(clip_count, seq_len, model_width)

    def split_rows(array):
        return jnp.transpose(array.reshape(clip_count, seq_len, head_count, DH), (0, 2, 1, 3)).reshape(clip_count * head_count, seq_len, DH)

    def merge_rows(array):
        return jnp.transpose(array.reshape(clip_count, head_count, seq_len, DH), (0, 2, 1, 3)).reshape(clip_count, seq_len, half_width)
    row_inputs = (split_rows(queries[..., :half_width]), split_rows(keys[..., :half_width]), split_rows(values[..., :half_width]), split_rows(attention_grad[..., :half_width]))
    row_results = lax.map(lambda item: row_item(item, score_scale), row_inputs)
    row_parts = [merge_rows(entry) for entry in row_results]
    blocks = seq_len // STRIDE

    def split_cols(array):
        shaped = array.reshape(clip_count, blocks, STRIDE, head_count, DH)
        return jnp.transpose(shaped, (0, 2, 3, 1, 4)).reshape(clip_count * STRIDE * head_count, blocks, DH)

    def merge_cols(array):
        shaped = array.reshape(clip_count, STRIDE, head_count, blocks, DH)
        return jnp.transpose(shaped, (0, 3, 1, 2, 4)).reshape(clip_count, seq_len, half_width)
    lower = lax.broadcasted_iota(jnp.int32, (blocks, blocks), 0) >= lax.broadcasted_iota(jnp.int32, (blocks, blocks), 1)
    col_results = attend(split_cols(queries[..., half_width:]), split_cols(keys[..., half_width:]), split_cols(values[..., half_width:]), split_cols(attention_grad[..., half_width:]), lower, score_scale)
    col_parts = [merge_cols(col_results[0]), merge_cols(col_results[1]), merge_cols(col_results[2].astype(jnp.bfloat16)), merge_cols(col_results[3].astype(jnp.bfloat16))]
    attention = jnp.concatenate([row_parts[0], col_parts[0]], axis=-1)
    query_grad = jnp.concatenate([row_parts[1], col_parts[1]], axis=-1)
    key_grad = jnp.concatenate([row_parts[2], col_parts[2]], axis=-1)
    value_grad = jnp.concatenate([row_parts[3], col_parts[3]], axis=-1)
    attn_flat = attention.reshape(clip_count * seq_len, model_width)
    layer_out = jnp.dot(attn_flat, w_out, preferred_element_type=jnp.float32).astype(jnp.bfloat16).reshape(clip_count, seq_len, model_width)
    weight_grad = jnp.dot(attn_flat.T, grad_flat, preferred_element_type=jnp.float32) * (1.0 / math.sqrt(clip_count * seq_len))
    return (layer_out, query_grad, key_grad, value_grad, weight_grad)
```

```python
import functools
import math

import jax
import jax.numpy as jnp
from jax import lax
from jax.experimental import pallas as pl
from jax.experimental.pallas import tpu as pltpu
from jax.sharding import Mesh
from jax.sharding import PartitionSpec as P

DH = 64
STRIDE = 1024
LANES = 128
BF16 = jnp.bfloat16
F32 = jnp.float32
SCALE = 1.0 / math.sqrt(DH)
SCALE_LOG2 = SCALE / math.log(2.0)
NT = (((1,), (1,)), ((), ()))
NN = (((1,), (0,)), ((), ()))
VMEM = pl.BlockSpec(memory_space=pltpu.VMEM)
SMEM = pl.BlockSpec(memory_space=pltpu.SMEM)


def dot(a, b, dims=NN):
    return lax.dot_general(a, b, dims, preferred_element_type=F32)


def call(kernel, out_shape, args, scratch=(), flops=0, vmem=32 << 20, smem=0):
    moved = sum(a.size * a.dtype.itemsize for a in args)
    outs = out_shape if isinstance(out_shape, tuple) else (out_shape,)
    moved += sum(math.prod(o.shape) * o.dtype.itemsize for o in outs)
    return pl.pallas_call(
        kernel,
        out_shape=out_shape,
        in_specs=[SMEM] * smem + [VMEM] * (len(args) - smem),
        out_specs=jax.tree.map(lambda _: VMEM, out_shape),
        scratch_shapes=list(scratch),
        compiler_params=pltpu.CompilerParams(vmem_limit_bytes=vmem),
        cost_estimate=pl.CostEstimate(flops=flops, bytes_accessed=moved, transcendentals=0),
    )(*args)


def shape(*dims, dtype=BF16):
    return jax.ShapeDtypeStruct(dims, dtype)


def low_half(rows):
    return lax.broadcasted_iota(jnp.int32, (rows, LANES), 1) < DH


def swap(tile):
    return pltpu.roll(tile, DH, 1)


def paired(a, b, low):
    a, b = a.astype(F32), b.astype(F32)
    first = jnp.where(low, a, swap(b))
    second = jnp.where(low, swap(a), b)
    return first.astype(BF16), second.astype(BF16)


def pack_kernel(q_ref, k_ref, v_ref, og_ref, w_ref, row_ref, col_ref):
    tokens, width = q_ref.shape
    heads = width // DH // 2
    part = tokens // col_ref.shape[0]
    low = low_half(tokens)
    grad = dot(og_ref[...], w_ref[...], NT).astype(BF16)
    for tile in range(heads):
        cut = slice(tile * LANES, (tile + 1) * LANES)
        kv = paired(k_ref[:, cut], v_ref[:, cut], low)
        qg = paired(q_ref[:, cut], grad[:, cut], low)
        for half in range(2):
            head = 2 * tile + half
            if head < heads:
                row_ref[head, :tokens] = kv[half]
                row_ref[head, tokens:] = qg[half]
            else:
                lanes = slice((head - heads) * LANES, (head - heads + 1) * LANES)
                for member in range(col_ref.shape[0]):
                    rows = slice(member * part, (member + 1) * part)
                    col_ref[member, :part, lanes] = kv[half][rows]
                    col_ref[member, part:, lanes] = qg[half][rows]


def split_diag(qg, low):
    zero = jnp.zeros_like(qg)
    return jnp.concatenate([jnp.where(low, qg, zero), jnp.where(low, zero, qg)], axis=0)


def col_kernel(in_ref, out_ref):
    blocks, rows, width = in_ref.shape
    part = rows // 2
    tokens = blocks * part
    low = low_half(tokens)
    key = lax.broadcasted_iota(jnp.int32, (tokens, tokens), 0)
    query = lax.broadcasted_iota(jnp.int32, (tokens, tokens), 1)
    allowed = (key <= query) & (((query - key) & (part - 1)) == 0)
    for head in range(width // LANES):
        cut = slice(head * LANES, (head + 1) * LANES)
        kv = in_ref[:, :part, cut].reshape(tokens, LANES)
        qg = in_ref[:, part:, cut].reshape(tokens, LANES)
        diag = split_diag(qg, low)
        both = dot(kv, diag, NT)
        score = jnp.where(allowed, both[:, :tokens] * SCALE_LOG2, -jnp.inf)
        weight = jnp.exp2(score - jnp.max(score, axis=0, keepdims=True))
        prob = weight / jnp.sum(weight, axis=0, keepdims=True)
        grad = both[:, tokens:]
        delta = jnp.sum(prob * grad, axis=0, keepdims=True)
        score_grad = prob * (grad - delta) * SCALE
        pair = jnp.concatenate([score_grad.astype(BF16), prob.astype(BF16)], axis=1)
        kv_grad = dot(pair, diag).astype(BF16)
        kv_t = kv.astype(F32).T.astype(BF16)
        flat = dot(kv_t, pair)
        back = jnp.concatenate([flat[:DH, :tokens], flat[DH:, tokens:]], axis=0)
        back = back.T.astype(BF16)
        out_ref[:, :part, cut] = back.reshape(blocks, part, LANES)
        out_ref[:, part:, cut] = kv_grad.reshape(blocks, part, LANES)


def row_kernel(first_ref, in_ref, prev_ref, out_ref, kv, kv_t, acc, score, grad, pair):
    tiles = in_ref.shape[0]
    size = in_ref.shape[1] // 2
    span = tiles * size
    chunks = tiles + 1
    low = low_half(size)
    bias = jnp.where(first_ref[0] == 0, -jnp.inf, 0.0).astype(F32)
    for tile in range(tiles):
        own = in_ref[tile, :size]
        before = prev_ref[tile]
        kv[span + tile * size : span + (tile + 1) * size] = own
        kv[tile * size : (tile + 1) * size] = before
        kv_t[:, span + tile * size : span + (tile + 1) * size] = own.astype(F32).T.astype(BF16)
        kv_t[:, tile * size : (tile + 1) * size] = before.astype(F32).T.astype(BF16)
    acc[...] = jnp.zeros_like(acc)
    key = lax.broadcasted_iota(jnp.int32, (size, size), 0)
    query = lax.broadcasted_iota(jnp.int32, (size, size), 1)
    for tile in range(tiles):
        base = tile * size
        diag = split_diag(in_ref[tile, size:], low)
        top = None
        for chunk in range(chunks):
            at = slice(base + chunk * size, base + (chunk + 1) * size)
            rows = slice(chunk * size, (chunk + 1) * size)
            both = dot(kv[at], diag, NT)
            now = both[:, :size] * SCALE_LOG2
            if chunk == 0:
                now = jnp.where(key > query, now, -jnp.inf)
            if chunk == chunks - 1:
                now = jnp.where(key <= query, now, -jnp.inf)
            if tile + chunk < tiles:
                now = now + bias
            score[rows] = now
            grad[rows] = both[:, size:]
            best = jnp.max(now, axis=0, keepdims=True)
            top = best if top is None else jnp.maximum(top, best)
        total = jnp.zeros((1, size), F32)
        inner = jnp.zeros((1, size), F32)
        for chunk in range(chunks):
            rows = slice(chunk * size, (chunk + 1) * size)
            weight = jnp.exp2(score[rows] - top)
            score[rows] = weight
            total = total + jnp.sum(weight, axis=0, keepdims=True)
            inner = inner + jnp.sum(weight * grad[rows], axis=0, keepdims=True)
        scaled = 1.0 / total
        delta = inner * scaled
        for chunk in range(chunks):
            rows = slice(chunk * size, (chunk + 1) * size)
            prob = score[rows] * scaled
            pair[rows, :size] = (prob * (grad[rows] - delta) * SCALE).astype(BF16)
            pair[rows, size:] = prob.astype(BF16)
        window = slice(base, base + chunks * size)
        acc[window] += dot(pair[...], diag)
        flat = dot(kv_t[:, window], pair[...])
        back = jnp.concatenate([flat[:DH, :size], flat[DH:, size:]], axis=0)
        out_ref[tile, :size] = back.T.astype(BF16)
    for tile in range(tiles):
        out_ref[tile, size : 2 * size] = acc[span + tile * size : span + (tile + 1) * size].astype(
            BF16
        )
        out_ref[tile, 2 * size :] = acc[tile * size : (tile + 1) * size].astype(BF16)


def unpaired(first, second, low):
    first, second = first.astype(F32), second.astype(F32)
    return jnp.where(low, first, swap(second)), jnp.where(low, swap(first), second)


def attention_kernel(row_ref, col_ref, att_ref, att_t_ref, dq_ref, prev_ref, turned):
    heads = row_ref.shape[0]
    tokens = row_ref.shape[1] // 3
    part = col_ref.shape[1] // 2
    groups, share, _ = att_t_ref.shape
    low = low_half(tokens)

    def one(head):
        if head < heads:
            return row_ref[head, :tokens]
        cut = slice((head - heads) * LANES, (head - heads + 1) * LANES)
        return col_ref[:, :part, cut].reshape(tokens, LANES)

    for tile in range(heads):
        cut = slice(tile * LANES, (tile + 1) * LANES)
        dq, att = unpaired(one(2 * tile), one(2 * tile + 1), low)
        dq_ref[:, cut] = dq.astype(BF16)
        att_ref[:, cut] = att.astype(BF16)
        turned[cut] = att.T
    for group in range(groups):
        att_t_ref[group] = turned[pl.ds(group, share, stride=groups)].astype(BF16)
    for head in range(heads):
        prev_ref[head] = row_ref[head, 2 * tokens :]


def layer_kernel(att_ref, w_ref, out_ref):
    out_ref[...] = dot(att_ref[...], w_ref[...]).astype(BF16)


def kv_grad_kernel(row_ref, col_ref, later_ref, dk_ref, dv_ref):
    heads = row_ref.shape[0]
    tokens = row_ref.shape[1] // 3
    part = col_ref.shape[1] // 2
    low = low_half(tokens)

    def one(head):
        if head < heads:
            own = row_ref[head, tokens : 2 * tokens].astype(F32)
            return own + later_ref[head].astype(F32)
        cut = slice((head - heads) * LANES, (head - heads + 1) * LANES)
        return col_ref[:, part:, cut].reshape(tokens, LANES)

    for tile in range(heads):
        cut = slice(tile * LANES, (tile + 1) * LANES)
        dk, dv = unpaired(one(2 * tile), one(2 * tile + 1), low)
        dk_ref[:, cut] = dk.astype(BF16)
        dv_ref[:, cut] = dv.astype(BF16)


def weight_kernel(me_ref, att_ref, own_ref, *rest):
    out_ref = rest[-1]
    me = me_ref[0]
    total = dot(att_ref[me], own_ref[...])
    for hop, grad_ref in enumerate(rest[:-1]):
        total = total + dot(att_ref[me ^ (hop + 1)], grad_ref[...])
    out_ref[...] = total.astype(BF16)


def swapped(array, axes):
    return lax.all_to_all(array, axes, split_axis=0, concat_axis=0, tiled=True)


def on_device(queries, keys, values, out_grad, w_out):
    _, tokens, width = queries.shape
    row_axes, plane_axes, line_axes = ("yl", "z"), ("b", "yl"), ("d", "z")
    clips, blocks = lax.axis_size("d"), lax.axis_size("b")
    lines = lax.axis_size("z")
    members = lax.axis_size("yl") * lines
    planes = blocks * lax.axis_size("yl")
    positions = blocks * members
    heads = width // DH // 2
    part = tokens // blocks
    q, k, v, og = (a.reshape(tokens, width) for a in (queries, keys, values, out_grad))
    block_index = lax.axis_index("b").astype(jnp.int32).reshape(1)
    clip_index = lax.axis_index("d").astype(jnp.int32).reshape(1)

    project = 2 * tokens * width * width
    row_in, col_in = call(
        pack_kernel,
        (shape(heads, 2 * tokens, LANES), shape(blocks, 2 * part, heads * LANES)),
        (q, k, v, og, w_out),
        flops=project,
    )
    row_got = swapped(row_in, row_axes)
    onward = [(i, i + 1) for i in range(blocks - 1)]
    prev = lax.ppermute(row_got[:, :tokens], "b", onward)
    col_got = swapped(col_in, "b")
    other_grads = [
        lax.ppermute(og, "d", [(i, i ^ hop) for i in range(clips)]) for hop in range(1, clips)
    ]
    col_res = call(
        col_kernel,
        shape(blocks, 2 * part, heads * LANES),
        (col_got,),
        flops=heads * 12 * tokens * tokens * LANES,
    )
    col_back = swapped(col_res, "b")
    span = members * tokens
    window = span + tokens
    row_res = call(
        row_kernel,
        shape(members, 3 * tokens, LANES),
        (block_index, row_got, prev),
        scratch=(
            pltpu.VMEM((2 * span, LANES), BF16),
            pltpu.VMEM((LANES, 2 * span), BF16),
            pltpu.VMEM((2 * span, LANES), F32),
            pltpu.VMEM((window, tokens), F32),
            pltpu.VMEM((window, tokens), F32),
            pltpu.VMEM((window, 2 * tokens), BF16),
        ),
        flops=members * 12 * window * tokens * LANES,
        smem=1,
    )
    row_back = swapped(row_res, row_axes)
    share = width // clips
    att, att_t, query_grad, before = call(
        attention_kernel,
        (
            shape(tokens, width),
            shape(clips, share, tokens),
            shape(tokens, width),
            shape(heads, tokens, LANES),
        ),
        (row_back, col_back),
        scratch=(pltpu.VMEM((width, tokens), F32),),
    )
    att_got = swapped(att_t, "d")
    later = lax.ppermute(before, "b", [(j, i) for i, j in onward])
    layer_out = call(layer_kernel, shape(tokens, width), (att, w_out), flops=project)
    key_grad, value_grad = call(
        kv_grad_kernel,
        (shape(tokens, width), shape(tokens, width)),
        (row_back, col_back, later),
    )
    partial = call(
        weight_kernel,
        shape(share, width),
        (clip_index, att_got, og, *other_grads),
        flops=project,
        smem=1,
    )
    piece = share // planes
    kept = piece // lines
    partial = swapped(partial.reshape(planes, piece, width), plane_axes)
    summed = jnp.sum(partial.astype(F32), axis=0).astype(BF16)
    sent = jnp.broadcast_to(summed.reshape(1, lines, kept, width), (clips, lines, kept, width))
    got = swapped(sent.reshape(clips * lines, kept, width), line_axes)
    total = jnp.sum(got.reshape(clips, lines, kept, width).astype(F32), axis=1)
    total = jnp.transpose(total, (1, 0, 2)).reshape(kept * clips, width)
    weight_grad = total * (1.0 / math.sqrt(clips * tokens * positions))
    whole = (1, tokens, width)
    return (
        layer_out.reshape(whole),
        query_grad.reshape(whole),
        key_grad.reshape(whole),
        value_grad.reshape(whole),
        weight_grad,
    )


def solution(mesh):
    clips, positions = mesh.devices.shape
    members = 8
    lines = 4
    split = (clips, positions // members, members // lines, lines)
    inner = Mesh(mesh.devices.reshape(split), ("d", "b", "yl", "z"))
    ctx = ("b", "yl", "z")
    placed = P("d", ctx, None)
    return jax.shard_map(
        on_device,
        mesh=inner,
        in_specs=(placed, placed, placed, placed, P()),
        out_specs=(placed, placed, placed, placed, P(ctx, None)),
        check_vma=False,
    )
```

```python
import functools
import math

import jax
import jax.numpy as jnp
from jax import lax
from jax.experimental import pallas as pl
from jax.experimental.pallas import tpu as pltpu
from jax.sharding import Mesh
from jax.sharding import PartitionSpec as P

DH = 64
STRIDE = 1024
LANES = 128
BF16 = jnp.bfloat16
F32 = jnp.float32
ROOM = 60 << 20
SCALE = 1.0 / math.sqrt(DH)
SCALE_LOG2 = SCALE / math.log(2.0)
NT = (((1,), (1,)), ((), ()))
NN = (((1,), (0,)), ((), ()))
VMEM = pl.BlockSpec(memory_space=pltpu.VMEM)
SMEM = pl.BlockSpec(memory_space=pltpu.SMEM)
HBM = pl.BlockSpec(memory_space=pltpu.HBM)


def dot(a, b, dims=NN):
    return lax.dot_general(a, b, dims, preferred_element_type=F32)


def call(kernel, out_shape, args, scratch=(), flops=0, vmem=32 << 20, specs=None):
    moved = sum(a.size * a.dtype.itemsize for a in args)
    outs = out_shape if isinstance(out_shape, tuple) else (out_shape,)
    moved += sum(math.prod(o.shape) * o.dtype.itemsize for o in outs)
    return pl.pallas_call(
        kernel,
        out_shape=out_shape,
        in_specs=specs or [VMEM] * len(args),
        out_specs=jax.tree.map(lambda _: VMEM, out_shape),
        scratch_shapes=list(scratch),
        compiler_params=pltpu.CompilerParams(vmem_limit_bytes=vmem),
        cost_estimate=pl.CostEstimate(flops=flops, bytes_accessed=moved, transcendentals=0),
    )(*args)


def shape(*dims, dtype=BF16):
    return jax.ShapeDtypeStruct(dims, dtype)


def low_half(rows):
    return lax.broadcasted_iota(jnp.int32, (rows, LANES), 1) < DH


def swap(tile):
    return pltpu.roll(tile, DH, 1)


def paired(a, b, low):
    a, b = a.astype(F32), b.astype(F32)
    first = jnp.where(low, a, swap(b))
    second = jnp.where(low, swap(a), b)
    return first.astype(BF16), second.astype(BF16)


def pack_kernel(flip_ref, q_hbm, k_hbm, v_hbm, og_hbm, w_hbm, row_ref, col_ref, *scratch):
    *held, sems = scratch
    copies = [
        pltpu.make_async_copy(source, target, sems.at[i])
        for i, (source, target) in enumerate(zip((og_hbm, w_hbm, k_hbm, v_hbm, q_hbm), held))
    ]
    for copy in copies:
        copy.start()
    og_ref, w_ref, k_ref, v_ref, q_ref = held
    tokens, width = q_ref.shape
    heads = width // DH // 2
    part = tokens // col_ref.shape[0]
    low = low_half(tokens)
    for copy in copies:
        copy.wait()
    grad = dot(og_ref[...], w_ref[...], NT).astype(BF16)
    for tile in range(heads):
        cut = slice(tile * LANES, (tile + 1) * LANES)
        kv = paired(k_ref[:, cut], v_ref[:, cut], low)
        qg = paired(q_ref[:, cut], grad[:, cut], low)
        for half in range(2):
            head = 2 * tile + half
            if head < heads:
                slot = head ^ flip_ref[0]
                row_ref[slot, :tokens] = kv[half]
                row_ref[slot, tokens:] = qg[half]
            else:
                lanes = slice((head - heads) * LANES, (head - heads + 1) * LANES)
                for member in range(col_ref.shape[0]):
                    rows = slice(member * part, (member + 1) * part)
                    col_ref[member, :part, lanes] = kv[half][rows]
                    col_ref[member, part:, lanes] = qg[half][rows]


def split_diag(qg, low):
    zero = jnp.zeros_like(qg)
    return jnp.concatenate([jnp.where(low, qg, zero), jnp.where(low, zero, qg)], axis=0)


def col_kernel(in_ref, out_ref):
    blocks, rows, width = in_ref.shape
    part = rows // 2
    tokens = blocks * part
    low = low_half(tokens)
    key = lax.broadcasted_iota(jnp.int32, (tokens, tokens), 0)
    query = lax.broadcasted_iota(jnp.int32, (tokens, tokens), 1)
    allowed = (key <= query) & (((query - key) & (part - 1)) == 0)
    for head in range(width // LANES):
        cut = slice(head * LANES, (head + 1) * LANES)
        kv = in_ref[:, :part, cut].reshape(tokens, LANES)
        qg = in_ref[:, part:, cut].reshape(tokens, LANES)
        diag = split_diag(qg, low)
        both = dot(kv, diag, NT)
        score = jnp.where(allowed, both[:, :tokens] * SCALE_LOG2, -jnp.inf)
        weight = jnp.exp2(score - jnp.max(score, axis=0, keepdims=True))
        prob = weight / jnp.sum(weight, axis=0, keepdims=True)
        grad = both[:, tokens:]
        delta = jnp.sum(prob * grad, axis=0, keepdims=True)
        score_grad = prob * (grad - delta) * SCALE
        pair = jnp.concatenate([score_grad.astype(BF16), prob.astype(BF16)], axis=1)
        kv_grad = dot(pair, diag).astype(BF16)
        kv_t = kv.astype(F32).T.astype(BF16)
        flat = dot(kv_t, pair)
        back = jnp.concatenate([flat[:DH, :tokens], flat[DH:, tokens:]], axis=0)
        back = back.T.astype(BF16)
        out_ref[:, :part, cut] = back.reshape(blocks, part, LANES)
        out_ref[:, part:, cut] = kv_grad.reshape(blocks, part, LANES)


def row_kernel(first_ref, in_ref, prev_ref, out_ref, kv, kv_t, acc, score, grad, pair):
    tiles = in_ref.shape[0]
    size = in_ref.shape[1] // 2
    span = tiles * size
    chunks = tiles + 1
    low = low_half(size)
    bias = jnp.where(first_ref[0] == 0, -jnp.inf, 0.0).astype(F32)
    for tile in range(tiles):
        own = in_ref[tile, :size]
        before = prev_ref[tile]
        kv[span + tile * size : span + (tile + 1) * size] = own
        kv[tile * size : (tile + 1) * size] = before
        kv_t[:, span + tile * size : span + (tile + 1) * size] = own.astype(F32).T.astype(BF16)
        kv_t[:, tile * size : (tile + 1) * size] = before.astype(F32).T.astype(BF16)
    acc[...] = jnp.zeros_like(acc)
    key = lax.broadcasted_iota(jnp.int32, (size, size), 0)
    query = lax.broadcasted_iota(jnp.int32, (size, size), 1)
    for tile in range(tiles):
        base = tile * size
        diag = split_diag(in_ref[tile, size:], low)
        top = None
        for chunk in range(chunks):
            at = slice(base + chunk * size, base + (chunk + 1) * size)
            rows = slice(chunk * size, (chunk + 1) * size)
            both = dot(kv[at], diag, NT)
            now = both[:, :size] * SCALE_LOG2
            if chunk == 0:
                now = jnp.where(key > query, now, -jnp.inf)
            if chunk == chunks - 1:
                now = jnp.where(key <= query, now, -jnp.inf)
            if tile + chunk < tiles:
                now = now + bias
            score[rows] = now
            grad[rows] = both[:, size:]
            best = jnp.max(now, axis=0, keepdims=True)
            top = best if top is None else jnp.maximum(top, best)
        total = jnp.zeros((1, size), F32)
        inner = jnp.zeros((1, size), F32)
        for chunk in range(chunks):
            rows = slice(chunk * size, (chunk + 1) * size)
            weight = jnp.exp2(score[rows] - top)
            score[rows] = weight
            total = total + jnp.sum(weight, axis=0, keepdims=True)
            inner = inner + jnp.sum(weight * grad[rows], axis=0, keepdims=True)
        scaled = 1.0 / total
        delta = inner * scaled
        for chunk in range(chunks):
            rows = slice(chunk * size, (chunk + 1) * size)
            prob = score[rows] * scaled
            pair[rows, :size] = (prob * (grad[rows] - delta) * SCALE).astype(BF16)
            pair[rows, size:] = prob.astype(BF16)
        window = slice(base, base + chunks * size)
        acc[window] += dot(pair[...], diag)
        flat = dot(kv_t[:, window], pair[...])
        back = jnp.concatenate([flat[:DH, :size], flat[DH:, size:]], axis=0)
        out_ref[tile, :size] = back.T.astype(BF16)
    for tile in range(tiles):
        out_ref[tile, size : 2 * size] = acc[span + tile * size : span + (tile + 1) * size].astype(
            BF16
        )
        out_ref[tile, 2 * size :] = acc[tile * size : (tile + 1) * size].astype(BF16)


def unpaired(first, second, low):
    first, second = first.astype(F32), second.astype(F32)
    return jnp.where(low, first, swap(second)), jnp.where(low, swap(first), second)


def packed_head(flip_ref, row_ref, col_ref, head, which):
    heads = row_ref.shape[0]
    tokens = row_ref.shape[1] // 3
    part = col_ref.shape[1] // 2
    if head < heads:
        return row_ref[head ^ flip_ref[0], which * tokens : (which + 1) * tokens]
    cut = slice((head - heads) * LANES, (head - heads + 1) * LANES)
    return col_ref[:, which * part : (which + 1) * part, cut].reshape(tokens, LANES)


def turn_kernel(flip_ref, me_ref, row_ref, col_ref, *rest):
    outs, turned = rest[:-1], rest[-1]
    heads = row_ref.shape[0]
    groups = len(outs)
    share, tokens = outs[0].shape
    low = low_half(tokens)
    for tile in range(heads):
        first = packed_head(flip_ref, row_ref, col_ref, 2 * tile, 0).astype(F32)
        second = packed_head(flip_ref, row_ref, col_ref, 2 * tile + 1, 0).astype(F32)
        att = jnp.where(low, swap(first), second)
        turned[tile * LANES : (tile + 1) * LANES] = att.T
    for hop, out_ref in enumerate(outs):
        out_ref[...] = turned[pl.ds(me_ref[0] ^ hop, share, stride=groups)].astype(BF16)


def layer_kernel(flip_ref, row_ref, col_ref, w_ref, out_ref, dq_ref, att):
    heads = row_ref.shape[0]
    low = low_half(att.shape[0])
    for tile in range(heads):
        cut = slice(tile * LANES, (tile + 1) * LANES)
        first = packed_head(flip_ref, row_ref, col_ref, 2 * tile, 0)
        second = packed_head(flip_ref, row_ref, col_ref, 2 * tile + 1, 0)
        dq, out = unpaired(first, second, low)
        dq_ref[:, cut] = dq.astype(BF16)
        att[:, cut] = out.astype(BF16)
    out_ref[...] = dot(att[...], w_ref[...]).astype(BF16)


def kv_grad_kernel(lines, flip_ref, row_ref, col_ref, later_ref, dk_ref, dv_ref):
    heads = row_ref.shape[0]
    low = low_half(dk_ref.shape[0])

    def one(head):
        mine = packed_head(flip_ref, row_ref, col_ref, head, 1)
        if head < heads:
            return mine.astype(F32) + later_ref[head ^ flip_ref[0] ^ lines].astype(F32)
        return mine

    for tile in range(heads):
        cut = slice(tile * LANES, (tile + 1) * LANES)
        dk, dv = unpaired(one(2 * tile), one(2 * tile + 1), low)
        dk_ref[:, cut] = dk.astype(BF16)
        dv_ref[:, cut] = dv.astype(BF16)


def weight_kernel(*refs):
    count = (len(refs) - 2) // 2
    sources, out_ref, held, sems = refs[:count], refs[count], refs[count + 1 : -1], refs[-1]
    copies = [
        pltpu.make_async_copy(source, target, sems.at[i])
        for i, (source, target) in enumerate(zip(sources, held))
    ]
    for copy in copies:
        copy.start()
    for copy in copies:
        copy.wait()
    half = count // 2
    total = None
    for att, grad in zip(held[:half], held[half:]):
        term = dot(att[...], grad[...])
        total = term if total is None else total + term
    out_ref[...] = total.astype(BF16).reshape(out_ref.shape)


def plane_sum_kernel(in_ref, out_ref):
    planes, piece, width = in_ref.shape
    pieces, rows, lanes = out_ref.shape
    kept = rows * lanes // width
    lines = piece // kept
    total = in_ref[0].astype(F32)
    for plane in range(1, planes):
        total = total + in_ref[plane].astype(F32)
    for line in range(lines):
        mine = total[line * kept : (line + 1) * kept]
        cuts = [mine[:, i * lanes : (i + 1) * lanes] for i in range(width // lanes)]
        packed = jnp.concatenate(cuts, axis=0).astype(BF16)
        for clip in range(pieces // lines):
            out_ref[clip * lines + line] = packed


def line_sum_kernel(clips, factor, in_ref, out_ref):
    pieces, rows, lanes = in_ref.shape
    lines = pieces // clips
    kept = out_ref.shape[0] // clips
    for clip in range(clips):
        total = in_ref[clip * lines].astype(F32)
        for line in range(1, lines):
            total = total + in_ref[clip * lines + line].astype(F32)
        total = total * factor
        for part in range(rows // kept):
            cut = slice(part * lanes, (part + 1) * lanes)
            for row in range(kept):
                at = part * kept + row
                to = row * clips + clip
                out_ref[to : to + 1, cut] = total[at : at + 1]


def swapped(array, axes):
    return lax.all_to_all(array, axes, split_axis=0, concat_axis=0, tiled=True)


def on_device(queries, keys, values, out_grad, w_out):
    _, tokens, width = queries.shape
    row_axes, plane_axes, line_axes = ("yl", "z"), ("b", "yl"), ("d", "z")
    clips, blocks = lax.axis_size("d"), lax.axis_size("b")
    lines = lax.axis_size("z")
    yl = lax.axis_size("yl")
    members = yl * lines
    planes = blocks * yl
    positions = blocks * members
    heads = width // DH // 2
    part = tokens // blocks
    q, k, v, og = (a.reshape(tokens, width) for a in (queries, keys, values, out_grad))
    block_index = lax.axis_index("b").astype(jnp.int32).reshape(1)
    clip_index = lax.axis_index("d").astype(jnp.int32).reshape(1)
    flip = (block_index & 1) * lines

    project = 2 * tokens * width * width
    row_in, col_in = call(
        pack_kernel,
        (shape(heads, 2 * tokens, LANES), shape(blocks, 2 * part, heads * LANES)),
        (flip, q, k, v, og, w_out),
        scratch=(
            pltpu.VMEM((tokens, width), BF16),
            pltpu.VMEM(w_out.shape, BF16),
            pltpu.VMEM((tokens, width), BF16),
            pltpu.VMEM((tokens, width), BF16),
            pltpu.VMEM((tokens, width), BF16),
            pltpu.SemaphoreType.DMA((5,)),
        ),
        flops=project,
        vmem=ROOM,
        specs=[SMEM] + [HBM] * 5,
    )
    row_got = swapped(row_in, row_axes)
    row_got, col_in, og_later = lax.optimization_barrier((row_got, col_in, og))
    onward = [
        (i * yl + j, (i + 1) * yl + j ^ 1) for i in range(blocks - 1) for j in range(yl)
    ]
    prev = lax.ppermute(row_got[:, :tokens], ("b", "yl"), onward)
    other_grads = [
        lax.ppermute(og_later, "d", [(i, i ^ hop) for i in range(clips)])
        for hop in range(1, clips)
    ]
    col_got = swapped(col_in, "b")
    col_got, prev = lax.optimization_barrier((col_got, prev))
    col_res = call(
        col_kernel,
        shape(blocks, 2 * part, heads * LANES),
        (col_got,),
        flops=heads * 12 * tokens * tokens * LANES,
    )
    col_back = swapped(col_res, "b")
    span = members * tokens
    window = span + tokens
    row_res = call(
        row_kernel,
        shape(members, 3 * tokens, LANES),
        (block_index, row_got, prev),
        scratch=(
            pltpu.VMEM((2 * span, LANES), BF16),
            pltpu.VMEM((LANES, 2 * span), BF16),
            pltpu.VMEM((2 * span, LANES), F32),
            pltpu.VMEM((window, tokens), F32),
            pltpu.VMEM((window, tokens), F32),
            pltpu.VMEM((window, 2 * tokens), BF16),
        ),
        flops=members * 12 * window * tokens * LANES,
        specs=[SMEM, VMEM, VMEM],
    )
    row_res, *other_grads = lax.optimization_barrier((row_res, *other_grads))
    row_back = swapped(row_res, row_axes)
    share = width // clips
    piece = share // planes
    kept = piece // lines
    turned = call(
        turn_kernel,
        (shape(share, tokens),) * clips,
        (flip, clip_index, row_back, col_back),
        scratch=(pltpu.VMEM((width, tokens), F32),),
        specs=[SMEM, SMEM, VMEM, VMEM],
    )
    att_got = [turned[0]] + [
        lax.ppermute(turned[hop], "d", [(i, i ^ hop) for i in range(clips)])
        for hop in range(1, clips)
    ]
    later = lax.ppermute(
        row_back[:, 2 * tokens :], "b", [(i + 1, i) for i in range(blocks - 1)]
    )
    layer_out, query_grad = call(
        layer_kernel,
        (shape(tokens, width), shape(tokens, width)),
        (flip, row_back, col_back, w_out),
        scratch=(pltpu.VMEM((tokens, width), BF16),),
        flops=project,
        specs=[SMEM, VMEM, VMEM, VMEM],
    )
    key_grad, value_grad = call(
        functools.partial(kv_grad_kernel, lines),
        (shape(tokens, width), shape(tokens, width)),
        (flip, row_back, col_back, later),
        specs=[SMEM, VMEM, VMEM, VMEM],
    )
    partial = call(
        weight_kernel,
        shape(planes, piece, width),
        (*att_got, og, *other_grads),
        scratch=(
            *[pltpu.VMEM((share, tokens), BF16)] * clips,
            *[pltpu.VMEM((tokens, width), BF16)] * clips,
            pltpu.SemaphoreType.DMA((2 * clips,)),
        ),
        flops=project,
        vmem=ROOM,
        specs=[HBM] * (2 * clips),
    )
    lanes = kept * width // piece
    summed = call(
        plane_sum_kernel,
        shape(clips * lines, piece, lanes),
        (swapped(partial, plane_axes),),
    )
    factor = 1.0 / math.sqrt(clips * tokens * positions)
    weight_grad = call(
        functools.partial(line_sum_kernel, clips, factor),
        shape(kept * clips, width, dtype=F32),
        (swapped(summed, line_axes),),
    )
    whole = (1, tokens, width)
    return (
        layer_out.reshape(whole),
        query_grad.reshape(whole),
        key_grad.reshape(whole),
        value_grad.reshape(whole),
        weight_grad,
    )


def solution(mesh):
    clips, positions = mesh.devices.shape
    members = 8
    lines = 4
    split = (clips, positions // members, members // lines, lines)
    inner = Mesh(mesh.devices.reshape(split), ("d", "b", "yl", "z"))
    ctx = ("b", "yl", "z")
    placed = P("d", ctx, None)
    return jax.shard_map(
        on_device,
        mesh=inner,
        in_specs=(placed, placed, placed, placed, P()),
        out_specs=(placed, placed, placed, placed, P(ctx, None)),
        check_vma=False,
    )
```

```python
import functools
import math

import jax
import jax.numpy as jnp
from jax import lax
from jax.experimental import pallas as pl
from jax.experimental.pallas import tpu as pltpu
from jax.sharding import Mesh
from jax.sharding import PartitionSpec as P

DH = 64
STRIDE = 1024
LANES = 128
BF16 = jnp.bfloat16
F32 = jnp.float32
ROOM = 60 << 20
EARLY = 7
SCALE = 1.0 / math.sqrt(DH)
SCALE_LOG2 = SCALE / math.log(2.0)
NT = (((1,), (1,)), ((), ()))
NN = (((1,), (0,)), ((), ()))
VMEM = pl.BlockSpec(memory_space=pltpu.VMEM)
SMEM = pl.BlockSpec(memory_space=pltpu.SMEM)
HBM = pl.BlockSpec(memory_space=pltpu.HBM)


def dot(a, b, dims=NN):
    return lax.dot_general(a, b, dims, preferred_element_type=F32)


def call(kernel, out_shape, args, scratch=(), flops=0, vmem=24 << 20, specs=None):
    moved = sum(a.size * a.dtype.itemsize for a in args)
    outs = out_shape if isinstance(out_shape, tuple) else (out_shape,)
    moved += sum(math.prod(o.shape) * o.dtype.itemsize for o in outs)
    return pl.pallas_call(
        kernel,
        out_shape=out_shape,
        in_specs=specs or [VMEM] * len(args),
        out_specs=jax.tree.map(lambda _: VMEM, out_shape),
        scratch_shapes=list(scratch),
        compiler_params=pltpu.CompilerParams(vmem_limit_bytes=vmem),
        cost_estimate=pl.CostEstimate(flops=flops, bytes_accessed=moved, transcendentals=0),
    )(*args)


def shape(*dims, dtype=BF16):
    return jax.ShapeDtypeStruct(dims, dtype)


def low_half(rows):
    return lax.broadcasted_iota(jnp.int32, (rows, LANES), 1) < DH


def swap(tile):
    return pltpu.roll(tile, DH, 1)


def paired(a, b, low):
    a, b = a.astype(F32), b.astype(F32)
    first = jnp.where(low, a, swap(b))
    second = jnp.where(low, swap(a), b)
    return first.astype(BF16), second.astype(BF16)


def fetch(pairs, sems):
    copies = [
        pltpu.make_async_copy(source, target, sems.at[i])
        for i, (source, target) in enumerate(pairs)
    ]
    for copy in copies:
        copy.start()
    for copy in copies:
        copy.wait()


def pack_row_kernel(flip_ref, q_hbm, k_hbm, v_hbm, og_hbm, w_hbm, row_ref, grad_ref, *scratch):
    og_ref, w_ref, k_ref, v_ref, q_ref, sems = scratch
    tokens = og_ref.shape[0]
    half = k_ref.shape[1]
    fetch(
        (
            (og_hbm, og_ref),
            (w_hbm, w_ref),
            (k_hbm.at[:, :half], k_ref),
            (v_hbm.at[:, :half], v_ref),
            (q_hbm.at[:, :half], q_ref),
        ),
        sems,
    )
    low = low_half(tokens)
    grad = dot(og_ref[...], w_ref[...], NT).astype(BF16)
    grad_ref[...] = grad[:, half:]
    for tile in range(half // LANES):
        cut = slice(tile * LANES, (tile + 1) * LANES)
        kv = paired(k_ref[:, cut], v_ref[:, cut], low)
        qg = paired(q_ref[:, cut], grad[:, cut], low)
        for side in range(2):
            slot = (2 * tile + side) ^ flip_ref[0]
            row_ref[slot, :tokens] = kv[side]
            row_ref[slot, tokens:] = qg[side]


def pack_col_kernel(me_ref, q_hbm, k_hbm, v_hbm, grad_hbm, *rest):
    count = len(rest) - 7
    outs = rest[:count]
    k_ref, v_ref, q_ref, grad_ref, kv_all, qg_all, sems = rest[count:]
    tokens, half = k_ref.shape
    part = tokens // count
    fetch(
        (
            (k_hbm.at[:, half:], k_ref),
            (v_hbm.at[:, half:], v_ref),
            (q_hbm.at[:, half:], q_ref),
            (grad_hbm, grad_ref),
        ),
        sems,
    )
    low = low_half(tokens)
    for tile in range(half // LANES):
        cut = slice(tile * LANES, (tile + 1) * LANES)
        kv = paired(k_ref[:, cut], v_ref[:, cut], low)
        qg = paired(q_ref[:, cut], grad_ref[:, cut], low)
        for side in range(2):
            lanes = slice((2 * tile + side) * LANES, (2 * tile + side + 1) * LANES)
            kv_all[:, lanes] = kv[side]
            qg_all[:, lanes] = qg[side]
    for hop, out_ref in enumerate(outs):
        rows = pl.ds(pl.multiple_of((me_ref[0] ^ hop) * part, part), part)
        out_ref[:part] = kv_all[rows]
        out_ref[part:] = qg_all[rows]


def split_diag(qg, low):
    zero = jnp.zeros_like(qg)
    return jnp.concatenate([jnp.where(low, qg, zero), jnp.where(low, zero, qg)], axis=0)


def col_kernel(me_ref, *rest):
    count = (len(rest) - 2) // 2
    sources, outs, held, sems = rest[:count], rest[count : 2 * count], rest[-2], rest[-1]
    fetch([(source, held.at[i]) for i, source in enumerate(sources)], sems)
    blocks, rows, width = held.shape
    part = rows // 2
    tokens = blocks * part
    low = low_half(tokens)
    key = lax.broadcasted_iota(jnp.int32, (tokens, tokens), 0)
    query = lax.broadcasted_iota(jnp.int32, (tokens, tokens), 1)
    flip = me_ref[0] * part
    allowed = ((key ^ flip) <= (query ^ flip)) & (((query ^ key) & (part - 1)) == 0)
    for head in range(width // LANES):
        cut = slice(head * LANES, (head + 1) * LANES)
        kv = held[:, :part, cut].reshape(tokens, LANES)
        qg = held[:, part:, cut].reshape(tokens, LANES)
        diag = split_diag(qg, low)
        both = dot(kv, diag, NT)
        score = jnp.where(allowed, both[:, :tokens] * SCALE_LOG2, -jnp.inf)
        weight = jnp.exp2(score - jnp.max(score, axis=0, keepdims=True))
        prob = weight / jnp.sum(weight, axis=0, keepdims=True)
        grad = both[:, tokens:]
        delta = jnp.sum(prob * grad, axis=0, keepdims=True)
        score_grad = prob * (grad - delta) * SCALE
        pair = jnp.concatenate([score_grad.astype(BF16), prob.astype(BF16)], axis=1)
        kv_grad = dot(pair, diag).astype(BF16)
        kv_t = kv.astype(F32).T.astype(BF16)
        flat = dot(kv_t, pair)
        back = jnp.concatenate([flat[:DH, :tokens], flat[DH:, tokens:]], axis=0)
        back = back.T.astype(BF16)
        for slot, out_ref in enumerate(outs):
            at = slice(slot * part, (slot + 1) * part)
            out_ref[:part, cut] = back[at]
            out_ref[part:, cut] = kv_grad[at]


def row_kernel(first_ref, in_hbm, prev_hbm, out_ref, kv, qg, kv_t, acc, score, grad, pair, sems):
    tiles, size, _ = qg.shape
    span = tiles * size
    chunks = tiles + 1
    low = low_half(size)
    bias = jnp.where(first_ref[0] == 0, -jnp.inf, 0.0).astype(F32)
    fetch(
        (
            (in_hbm.at[:, :size], kv.at[tiles:]),
            (in_hbm.at[:, size:], qg),
            (prev_hbm, kv.at[:tiles]),
        ),
        sems,
    )
    for block in range(2 * tiles):
        kv_t[:, block * size : (block + 1) * size] = kv[block].astype(F32).T.astype(BF16)
    acc[...] = jnp.zeros_like(acc)
    key = lax.broadcasted_iota(jnp.int32, (size, size), 0)
    query = lax.broadcasted_iota(jnp.int32, (size, size), 1)
    for tile in range(tiles):
        base = tile * size
        diag = split_diag(qg[tile], low)
        top = None
        for chunk in range(chunks):
            rows = slice(chunk * size, (chunk + 1) * size)
            both = dot(kv[tile + chunk], diag, NT)
            now = both[:, :size] * SCALE_LOG2
            if chunk == 0:
                now = jnp.where(key > query, now, -jnp.inf)
            if chunk == chunks - 1:
                now = jnp.where(key <= query, now, -jnp.inf)
            if tile + chunk < tiles:
                now = now + bias
            score[rows] = now
            grad[rows] = both[:, size:]
            best = jnp.max(now, axis=0, keepdims=True)
            top = best if top is None else jnp.maximum(top, best)
        total = jnp.zeros((1, size), F32)
        inner = jnp.zeros((1, size), F32)
        for chunk in range(chunks):
            rows = slice(chunk * size, (chunk + 1) * size)
            weight = jnp.exp2(score[rows] - top)
            score[rows] = weight
            total = total + jnp.sum(weight, axis=0, keepdims=True)
            inner = inner + jnp.sum(weight * grad[rows], axis=0, keepdims=True)
        scaled = 1.0 / total
        delta = inner * scaled
        for chunk in range(chunks):
            rows = slice(chunk * size, (chunk + 1) * size)
            prob = score[rows] * scaled
            pair[rows, :size] = (prob * (grad[rows] - delta) * SCALE).astype(BF16)
            pair[rows, size:] = prob.astype(BF16)
        window = slice(base, base + chunks * size)
        acc[window] += dot(pair[...], diag)
        flat = dot(kv_t[:, window], pair[...])
        back = jnp.concatenate([flat[:DH, :size], flat[DH:, size:]], axis=0)
        out_ref[tile, :size] = back.T.astype(BF16)
    for tile in range(tiles):
        out_ref[tile, size : 2 * size] = acc[span + tile * size : span + (tile + 1) * size].astype(
            BF16
        )
        out_ref[tile, 2 * size :] = acc[tile * size : (tile + 1) * size].astype(BF16)


def unpaired(first, second, low):
    first, second = first.astype(F32), second.astype(F32)
    return jnp.where(low, first, swap(second)), jnp.where(low, swap(first), second)


def fetch_packed(block_ref, row_hbm, col_hbms, row, col, sems, which):
    tokens, part = row.shape[1], col.shape[1]
    pairs = [(row_hbm.at[:, which * tokens : (which + 1) * tokens], row)]
    for hop, col_hbm in enumerate(col_hbms):
        source = col_hbm.at[which * part : (which + 1) * part]
        pairs.append((source, col.at[block_ref[0] ^ hop]))
    fetch(pairs, sems)


def packed_head(flip_ref, row, col, head):
    heads, tokens, _ = row.shape
    if head < heads:
        return row[head ^ flip_ref[0]]
    cut = slice((head - heads) * LANES, (head - heads + 1) * LANES)
    return col[:, :, cut].reshape(tokens, LANES)


def turn_kernel(clips, flip_ref, block_ref, me_ref, row_hbm, *rest):
    col_hbms, outs = rest[: -clips - 4], rest[-clips - 4 : -4]
    row, col, turned, sems = rest[-4:]
    fetch_packed(block_ref, row_hbm, col_hbms, row, col, sems, 0)
    share, tokens = outs[0].shape
    low = low_half(tokens)
    for tile in range(row.shape[0]):
        first = packed_head(flip_ref, row, col, 2 * tile).astype(F32)
        second = packed_head(flip_ref, row, col, 2 * tile + 1).astype(F32)
        att = jnp.where(low, swap(first), second)
        turned[tile * LANES : (tile + 1) * LANES] = att.T
    for hop, out_ref in enumerate(outs):
        out_ref[...] = turned[pl.ds(me_ref[0] ^ hop, share, stride=clips)].astype(BF16)


def layer_kernel(flip_ref, block_ref, w_hbm, row_hbm, *rest):
    col_hbms, out_ref, dq_ref = rest[:-7], rest[-7], rest[-6]
    row, col, att, w_ref, sems = rest[-5:]
    copy = pltpu.make_async_copy(w_hbm, w_ref, sems.at[len(col_hbms) + 1])
    copy.start()
    fetch_packed(block_ref, row_hbm, col_hbms, row, col, sems, 0)
    low = low_half(att.shape[0])
    for tile in range(row.shape[0]):
        cut = slice(tile * LANES, (tile + 1) * LANES)
        first = packed_head(flip_ref, row, col, 2 * tile)
        second = packed_head(flip_ref, row, col, 2 * tile + 1)
        dq, out = unpaired(first, second, low)
        dq_ref[:, cut] = dq.astype(BF16)
        att[:, cut] = out.astype(BF16)
    copy.wait()
    out_ref[...] = dot(att[...], w_ref[...]).astype(BF16)


def kv_grad_kernel(lines, flip_ref, block_ref, later_hbm, row_hbm, *rest):
    col_hbms, dk_ref, dv_ref = rest[:-6], rest[-6], rest[-5]
    row, col, later, sems = rest[-4:]
    copy = pltpu.make_async_copy(later_hbm, later, sems.at[len(col_hbms) + 1])
    copy.start()
    fetch_packed(block_ref, row_hbm, col_hbms, row, col, sems, 1)
    copy.wait()
    low = low_half(dk_ref.shape[0])

    def one(head):
        mine = packed_head(flip_ref, row, col, head)
        if head < row.shape[0]:
            return mine.astype(F32) + later[head ^ flip_ref[0] ^ lines].astype(F32)
        return mine

    for tile in range(row.shape[0]):
        cut = slice(tile * LANES, (tile + 1) * LANES)
        dk, dv = unpaired(one(2 * tile), one(2 * tile + 1), low)
        dk_ref[:, cut] = dk.astype(BF16)
        dv_ref[:, cut] = dv.astype(BF16)


def weight_kernel(*refs):
    count = (len(refs) - 4) // 2
    out_ref, att, grad, sems = refs[2 * count :]
    tokens = att.shape[1] // count
    pairs = []
    for i in range(count):
        at = pl.ds(i * tokens, tokens)
        pairs.append((refs[i], att.at[:, at]))
        pairs.append((refs[count + i], grad.at[at]))
    fetch(pairs, sems)
    out_ref[...] = dot(att[...], grad[...]).astype(BF16).reshape(out_ref.shape)


def plane_sum_kernel(in_ref, out_ref):
    planes, piece, width = in_ref.shape
    pieces, rows, lanes = out_ref.shape
    kept = rows * lanes // width
    lines = piece // kept
    total = in_ref[0].astype(F32)
    for plane in range(1, planes):
        total = total + in_ref[plane].astype(F32)
    for line in range(lines):
        mine = total[line * kept : (line + 1) * kept]
        cuts = [mine[:, i * lanes : (i + 1) * lanes] for i in range(width // lanes)]
        packed = jnp.concatenate(cuts, axis=0).astype(BF16)
        for clip in range(pieces // lines):
            out_ref[clip * lines + line] = packed


def line_sum_kernel(clips, factor, in_ref, out_ref):
    pieces, rows, lanes = in_ref.shape
    lines = pieces // clips
    kept = out_ref.shape[0] // clips
    for clip in range(clips):
        total = in_ref[clip * lines].astype(F32)
        for line in range(1, lines):
            total = total + in_ref[clip * lines + line].astype(F32)
        total = total * factor
        for part in range(rows // kept):
            cut = slice(part * lanes, (part + 1) * lanes)
            for row in range(kept):
                at = part * kept + row
                to = row * clips + clip
                out_ref[to : to + 1, cut] = total[at : at + 1]


def swapped(array, axes):
    return lax.all_to_all(array, axes, split_axis=0, concat_axis=0, tiled=True)


def on_device(queries, keys, values, out_grad, w_out):
    _, tokens, width = queries.shape
    row_axes, plane_axes, line_axes = ("yl", "z"), ("b", "yl"), ("d", "z")
    clips, blocks = lax.axis_size("d"), lax.axis_size("b")
    lines = lax.axis_size("z")
    yl = lax.axis_size("yl")
    members = yl * lines
    planes = blocks * yl
    positions = blocks * members
    heads = width // DH // 2
    part = tokens // blocks
    q, k, v, og = (a.reshape(tokens, width) for a in (queries, keys, values, out_grad))
    block_index = lax.axis_index("b").astype(jnp.int32).reshape(1)
    clip_index = lax.axis_index("d").astype(jnp.int32).reshape(1)
    flip = (block_index & 1) * lines

    project = 2 * tokens * width * width
    half = width // 2
    sems = pltpu.SemaphoreType.DMA
    row_in, grad_col = call(
        pack_row_kernel,
        (shape(heads, 2 * tokens, LANES), shape(tokens, half)),
        (flip, q, k, v, og, w_out),
        scratch=(
            pltpu.VMEM((tokens, width), BF16),
            pltpu.VMEM(w_out.shape, BF16),
            *[pltpu.VMEM((tokens, half), BF16)] * 3,
            sems((5,)),
        ),
        flops=project,
        vmem=ROOM,
        specs=[SMEM] + [HBM] * 5,
    )
    row_got = swapped(row_in, row_axes)
    col_piece = shape(2 * part, heads * LANES)
    col_in = call(
        pack_col_kernel,
        (col_piece,) * blocks,
        (block_index, q, k, v, grad_col),
        scratch=(
            *[pltpu.VMEM((tokens, half), BF16)] * 4,
            *[pltpu.VMEM((tokens, width), BF16)] * 2,
            sems((4,)),
        ),
        specs=[SMEM] + [HBM] * 4,
    )

    def to_members(pieces, hops):
        return [
            lax.ppermute(pieces[hop], "b", [(i, i ^ hop) for i in range(blocks)]) for hop in hops
        ]

    first, second = range(1, EARLY + 1), range(EARLY + 1, blocks)
    col_got = to_members(col_in, first)
    row_got, og_later, *rest = lax.optimization_barrier(
        (row_got, og, *col_got, *(col_in[hop] for hop in second))
    )
    col_got, col_wait = rest[:EARLY], dict(zip(second, rest[EARLY:]))
    onward = [(i * yl + j, (i + 1) * yl + j ^ 1) for i in range(blocks - 1) for j in range(yl)]
    prev = lax.ppermute(row_got[:, :tokens], ("b", "yl"), onward)
    col_got = [col_in[0], *col_got, *to_members(col_wait, second)]
    col_res = call(
        col_kernel,
        (col_piece,) * blocks,
        (block_index, *col_got),
        scratch=(pltpu.VMEM((blocks, 2 * part, heads * LANES), BF16), sems((blocks,))),
        flops=heads * 12 * tokens * tokens * LANES,
        specs=[SMEM] + [HBM] * blocks,
    )
    other_grads = [
        lax.ppermute(og_later, "d", [(i, i ^ hop) for i in range(clips)])
        for hop in range(1, clips)
    ]
    prev, col_res = lax.optimization_barrier((prev, col_res))
    span = members * tokens
    window = span + tokens
    row_res = call(
        row_kernel,
        shape(members, 3 * tokens, LANES),
        (block_index, row_got, prev),
        scratch=(
            pltpu.VMEM((2 * members, tokens, LANES), BF16),
            pltpu.VMEM((members, tokens, LANES), BF16),
            pltpu.VMEM((LANES, 2 * span), BF16),
            pltpu.VMEM((2 * span, LANES), F32),
            pltpu.VMEM((window, tokens), F32),
            pltpu.VMEM((window, tokens), F32),
            pltpu.VMEM((window, 2 * tokens), BF16),
            sems((3,)),
        ),
        flops=members * 12 * window * tokens * LANES,
        specs=[SMEM, HBM, HBM],
    )
    row_res, col_res, other_grads = lax.optimization_barrier((row_res, col_res, other_grads))
    row_back = swapped(row_res, row_axes)
    col_back = [col_res[0], *to_members(col_res, range(1, blocks))]
    share = width // clips
    piece = share // planes
    kept = piece // lines
    packed = (pltpu.VMEM((heads, tokens, LANES), BF16), pltpu.VMEM((blocks, part, width), BF16))
    turned = call(
        functools.partial(turn_kernel, clips),
        (shape(share, tokens),) * clips,
        (flip, block_index, clip_index, row_back, *col_back),
        scratch=(*packed, pltpu.VMEM((width, tokens), F32), sems((blocks + 1,))),
        specs=[SMEM] * 3 + [HBM] * (blocks + 1),
    )
    att_got = [turned[0]] + [
        lax.ppermute(turned[hop], "d", [(i, i ^ hop) for i in range(clips)])
        for hop in range(1, clips)
    ]
    later = lax.ppermute(
        row_back[:, 2 * tokens :], "b", [(i + 1, i) for i in range(blocks - 1)]
    )
    layer_out, query_grad = call(
        layer_kernel,
        (shape(tokens, width), shape(tokens, width)),
        (flip, block_index, w_out, row_back, *col_back),
        scratch=(
            *packed,
            pltpu.VMEM((tokens, width), BF16),
            pltpu.VMEM(w_out.shape, BF16),
            sems((blocks + 2,)),
        ),
        flops=project,
        specs=[SMEM] * 2 + [HBM] * (blocks + 2),
    )
    key_grad, value_grad = call(
        functools.partial(kv_grad_kernel, lines),
        (shape(tokens, width), shape(tokens, width)),
        (flip, block_index, later, row_back, *col_back),
        scratch=(
            *packed,
            pltpu.VMEM((heads, tokens, LANES), BF16),
            sems((blocks + 2,)),
        ),
        specs=[SMEM] * 2 + [HBM] * (blocks + 2),
    )
    att_got, layer_out = lax.optimization_barrier((att_got, layer_out))
    partial = call(
        weight_kernel,
        shape(planes, piece, width),
        (*att_got, og, *other_grads),
        scratch=(
            pltpu.VMEM((share, clips * tokens), BF16),
            pltpu.VMEM((clips * tokens, width), BF16),
            sems((2 * clips,)),
        ),
        flops=project,
        vmem=ROOM,
        specs=[HBM] * (2 * clips),
    )
    lanes = kept * width // piece
    summed = call(
        plane_sum_kernel,
        shape(clips * lines, piece, lanes),
        (swapped(partial, plane_axes),),
    )
    factor = 1.0 / math.sqrt(clips * tokens * positions)
    weight_grad = call(
        functools.partial(line_sum_kernel, clips, factor),
        shape(kept * clips, width, dtype=F32),
        (swapped(summed, line_axes),),
    )
    whole = (1, tokens, width)
    return (
        layer_out.reshape(whole),
        query_grad.reshape(whole),
        key_grad.reshape(whole),
        value_grad.reshape(whole),
        weight_grad,
    )


def solution(mesh):
    clips, positions = mesh.devices.shape
    members = 8
    lines = 4
    split = (clips, positions // members, members // lines, lines)
    inner = Mesh(mesh.devices.reshape(split), ("d", "b", "yl", "z"))
    ctx = ("b", "yl", "z")
    placed = P("d", ctx, None)
    return jax.shard_map(
        on_device,
        mesh=inner,
        in_specs=(placed, placed, placed, placed, P()),
        out_specs=(placed, placed, placed, placed, P(ctx, None)),
        check_vma=False,
    )
```

```python
import functools
import math

import jax
import jax.numpy as jnp
from jax import lax
from jax.experimental import pallas as pl
from jax.experimental.pallas import tpu as pltpu
from jax.sharding import Mesh
from jax.sharding import PartitionSpec as P

DH = 64
STRIDE = 1024
LANES = 128
BF16 = jnp.bfloat16
F32 = jnp.float32
ROOM = 60 << 20
SCALE = 1.0 / math.sqrt(DH)
SCALE_LOG2 = SCALE / math.log(2.0)
NT = (((1,), (1,)), ((), ()))
NN = (((1,), (0,)), ((), ()))
VMEM = pl.BlockSpec(memory_space=pltpu.VMEM)
SMEM = pl.BlockSpec(memory_space=pltpu.SMEM)
HBM = pl.BlockSpec(memory_space=pltpu.HBM)


def dot(a, b, dims=NN):
    return lax.dot_general(a, b, dims, preferred_element_type=F32)


def call(kernel, out_shape, args, scratch=(), flops=0, vmem=52 << 20, specs=None):
    moved = sum(a.size * a.dtype.itemsize for a in args)
    outs = out_shape if isinstance(out_shape, tuple) else (out_shape,)
    moved += sum(math.prod(o.shape) * o.dtype.itemsize for o in outs)
    return pl.pallas_call(
        kernel,
        out_shape=out_shape,
        in_specs=specs or [VMEM] * len(args),
        out_specs=jax.tree.map(lambda _: VMEM, out_shape),
        scratch_shapes=list(scratch),
        compiler_params=pltpu.CompilerParams(vmem_limit_bytes=vmem),
        cost_estimate=pl.CostEstimate(flops=flops, bytes_accessed=moved, transcendentals=0),
    )(*args)


def shape(*dims, dtype=BF16):
    return jax.ShapeDtypeStruct(dims, dtype)


def low_half(rows):
    return lax.broadcasted_iota(jnp.int32, (rows, LANES), 1) < DH


def swap(tile):
    return pltpu.roll(tile, DH, 1)


def paired(a, b, low):
    a, b = a.astype(F32), b.astype(F32)
    first = jnp.where(low, a, swap(b))
    second = jnp.where(low, swap(a), b)
    return first.astype(BF16), second.astype(BF16)


def fetch(pairs, sems):
    copies = [
        pltpu.make_async_copy(source, target, sems.at[i])
        for i, (source, target) in enumerate(pairs)
    ]
    for copy in copies:
        copy.start()
    for copy in copies:
        copy.wait()


def pack_kernel(
    flip_ref, me_ref, q_hbm, k_hbm, v_hbm, og_hbm, w_hbm, row_ref, *rest
):
    outs = rest[:-8]
    og_ref, w_ref, k_ref, v_ref, q_ref, kv_all, qg_all, sems = rest[-8:]
    tokens, width = og_ref.shape
    half = width // 2
    pairs = ((k_hbm, k_ref), (v_hbm, v_ref), (q_hbm, q_ref), (og_hbm, og_ref), (w_hbm, w_ref))
    copies = [
        pltpu.make_async_copy(source, target, sems.at[i])
        for i, (source, target) in enumerate(pairs)
    ]
    for copy in copies:
        copy.start()
    low = low_half(tokens)
    heads = half // DH

    def put(tile, one, two, rows, both):
        cut = slice(tile * LANES, (tile + 1) * LANES)
        for side, value in enumerate(paired(one[:, cut], two[:, cut], low)):
            head = 2 * tile + side
            if head < heads:
                row_ref[head ^ flip_ref[0], rows] = value
            else:
                both[:, (head - heads) * LANES : (head - heads + 1) * LANES] = value

    for copy in copies[:3]:
        copy.wait()
    for tile in range(width // LANES):
        put(tile, k_ref, v_ref, slice(0, tokens), kv_all)
    for copy in copies[3:]:
        copy.wait()
    og_ref[...] = dot(og_ref[...], w_ref[...], NT).astype(BF16)
    for tile in range(width // LANES):
        put(tile, q_ref, og_ref, slice(tokens, 2 * tokens), qg_all)
    part = tokens // len(outs)
    for slot, out_ref in enumerate(outs):
        rows = pl.ds(pl.multiple_of((me_ref[0] ^ slot) * part, part), part)
        out_ref[:part] = kv_all[rows]
        out_ref[part:] = qg_all[rows]


def split_diag(qg, low, factor=1.0):
    zero = jnp.zeros_like(qg)
    grad = qg * BF16(factor) if factor != 1.0 else qg
    return jnp.concatenate([jnp.where(low, qg, zero), jnp.where(low, zero, grad)], axis=0)


def col_kernel(me_ref, *rest):
    count = (len(rest) - 2) // 2
    sources, outs, held, sems = rest[:count], rest[count : 2 * count], rest[-2], rest[-1]
    fetch([(source, held.at[i]) for i, source in enumerate(sources)], sems)
    blocks, rows, width = held.shape
    part = rows // 2
    tokens = blocks * part
    low = low_half(tokens)
    key = lax.broadcasted_iota(jnp.int32, (tokens, tokens), 0)
    query = lax.broadcasted_iota(jnp.int32, (tokens, tokens), 1)
    flip = me_ref[0] * part
    allowed = ((key ^ flip) <= (query ^ flip)) & (((query ^ key) & (part - 1)) == 0)
    heads = range(width // LANES)
    cuts = [slice(head * LANES, (head + 1) * LANES) for head in heads]
    kvs = [held[:, :part, cut].reshape(tokens, LANES) for cut in cuts]
    qgs = [held[:, part:, cut].reshape(tokens, LANES) for cut in cuts]
    boths = [dot(kv, split_diag(qg, low, SCALE), NT) for kv, qg in zip(kvs, qgs)]
    pairs = []
    for both in boths:
        score = jnp.where(allowed, both[:, :tokens] * SCALE_LOG2, -jnp.inf)
        weight = jnp.exp2(score - jnp.max(score, axis=0, keepdims=True))
        grad = both[:, tokens:]
        scaled = 1.0 / jnp.sum(weight, axis=0, keepdims=True)
        prob = weight * scaled
        delta = jnp.sum(prob * grad, axis=0, keepdims=True)
        score_grad = prob * (grad - delta)
        pairs.append(jnp.concatenate([score_grad.astype(BF16), prob.astype(BF16)], axis=1))
    kv_grads = [dot(pair, split_diag(qg, low)).astype(BF16) for pair, qg in zip(pairs, qgs)]
    flats = [dot(kv.astype(F32).T.astype(BF16), pair) for kv, pair in zip(kvs, pairs)]
    for cut, flat, kv_grad in zip(cuts, flats, kv_grads):
        back = jnp.concatenate([flat[:DH, :tokens], flat[DH:, tokens:]], axis=0)
        back = back.T.astype(BF16)
        for slot, out_ref in enumerate(outs):
            at = slice(slot * part, (slot + 1) * part)
            out_ref[:part, cut] = back[at]
            out_ref[part:, cut] = kv_grad[at]


def row_kernel(first_ref, in_hbm, prev_hbm, out_ref, kv, qg, kv_t, acc, score, grad, pair, sems):
    tiles, size, _ = qg.shape
    span = tiles * size
    chunks = tiles + 1
    low = low_half(size)
    bias = jnp.where(first_ref[0] == 0, -jnp.inf, 0.0).astype(F32)
    fetch(
        (
            (in_hbm.at[:, :size], kv.at[tiles:]),
            (in_hbm.at[:, size:], qg),
            (prev_hbm, kv.at[:tiles]),
        ),
        sems,
    )
    acc[...] = jnp.zeros_like(acc)
    key = lax.broadcasted_iota(jnp.int32, (size, size), 0)
    query = lax.broadcasted_iota(jnp.int32, (size, size), 1)

    def turn(block):
        kv_t[:, block * size : (block + 1) * size] = kv[block].astype(F32).T.astype(BF16)

    def scores(tile):
        slot = tile % 2
        diag = split_diag(qg[tile], low, SCALE)
        top = None
        for chunk in range(chunks):
            rows = slice(chunk * size, (chunk + 1) * size)
            both = dot(kv[tile + chunk], diag, NT)
            now = both[:, :size] * SCALE_LOG2
            if chunk == 0:
                now = jnp.where(key > query, now, -jnp.inf)
            if chunk == chunks - 1:
                now = jnp.where(key <= query, now, -jnp.inf)
            if tile + chunk < tiles:
                now = now + bias
            score[slot, rows] = now
            grad[slot, rows] = both[:, size:]
            best = jnp.max(now, axis=0, keepdims=True)
            top = best if top is None else jnp.maximum(top, best)
        return top

    def softmax(tile, top):
        slot = tile % 2
        total = jnp.zeros((1, size), F32)
        inner = jnp.zeros((1, size), F32)
        for chunk in range(chunks):
            rows = slice(chunk * size, (chunk + 1) * size)
            weight = jnp.exp2(score[slot, rows] - top)
            score[slot, rows] = weight
            total = total + jnp.sum(weight, axis=0, keepdims=True)
            inner = inner + jnp.sum(weight * grad[slot, rows], axis=0, keepdims=True)
        scaled = 1.0 / total
        delta = inner * scaled
        for chunk in range(chunks):
            rows = slice(chunk * size, (chunk + 1) * size)
            prob = score[slot, rows] * scaled
            pair[slot, rows, :size] = (prob * (grad[slot, rows] - delta)).astype(BF16)
            pair[slot, rows, size:] = prob.astype(BF16)

    def products(tile):
        slot = tile % 2
        window = slice(tile * size, (tile + chunks) * size)
        acc[window] += dot(pair[slot], split_diag(qg[tile], low))
        flat = dot(kv_t[:, window], pair[slot])
        back = jnp.concatenate([flat[:DH, :size], flat[DH:, size:]], axis=0)
        out_ref[tile, :size] = back.T.astype(BF16)

    top = scores(0)
    for block in range(chunks):
        turn(block)
    for tile in range(tiles):
        later = scores(tile + 1) if tile + 1 < tiles else None
        softmax(tile, top)
        products(tile)
        if tile + 1 < tiles:
            turn(tile + chunks)
        top = later
    for tile in range(tiles):
        own = acc[span + tile * size : span + (tile + 1) * size]
        out_ref[tile, size : 2 * size] = own.astype(BF16)
        out_ref[tile, 2 * size :] = acc[tile * size : (tile + 1) * size].astype(BF16)


def unpaired(first, second, low):
    first, second = first.astype(F32), second.astype(F32)
    return jnp.where(low, first, swap(second)), jnp.where(low, swap(first), second)


def fetch_packed(block_ref, row_hbm, col_hbms, row, col, sems, which):
    tokens, part = row.shape[1], col.shape[1]
    pairs = [(row_hbm.at[:, which * tokens : (which + 1) * tokens], row)]
    for hop, col_hbm in enumerate(col_hbms):
        source = col_hbm.at[which * part : (which + 1) * part]
        pairs.append((source, col.at[block_ref[0] ^ hop]))
    fetch(pairs, sems)


def packed_head(flip_ref, row, col, head):
    heads, tokens, _ = row.shape
    if head < heads:
        return row[head ^ flip_ref[0]]
    cut = slice((head - heads) * LANES, (head - heads + 1) * LANES)
    return col[:, :, cut].reshape(tokens, LANES)


def turn_kernel(clips, flip_ref, block_ref, me_ref, row_hbm, *rest):
    col_hbms, outs = rest[: -clips - 4], rest[-clips - 4 : -4]
    row, col, turned, sems = rest[-4:]
    fetch_packed(block_ref, row_hbm, col_hbms, row, col, sems, 0)
    share, tokens = outs[0].shape
    low = low_half(tokens)
    for tile in range(row.shape[0]):
        first = packed_head(flip_ref, row, col, 2 * tile).astype(F32)
        second = packed_head(flip_ref, row, col, 2 * tile + 1).astype(F32)
        att = jnp.where(low, swap(first), second)
        turned[tile * LANES : (tile + 1) * LANES] = att.T
    for hop, out_ref in enumerate(outs):
        out_ref[...] = turned[pl.ds(me_ref[0] ^ hop, share, stride=clips)].astype(BF16)


def layer_kernel(flip_ref, block_ref, w_hbm, row_hbm, *rest):
    col_hbms, out_ref, dq_ref = rest[:-7], rest[-7], rest[-6]
    row, col, att, w_ref, sems = rest[-5:]
    copy = pltpu.make_async_copy(w_hbm, w_ref, sems.at[len(col_hbms) + 1])
    copy.start()
    fetch_packed(block_ref, row_hbm, col_hbms, row, col, sems, 0)
    low = low_half(att.shape[0])
    for tile in range(row.shape[0]):
        cut = slice(tile * LANES, (tile + 1) * LANES)
        first = packed_head(flip_ref, row, col, 2 * tile)
        second = packed_head(flip_ref, row, col, 2 * tile + 1)
        dq, out = unpaired(first, second, low)
        dq_ref[:, cut] = dq.astype(BF16)
        att[:, cut] = out.astype(BF16)
    copy.wait()
    out_ref[...] = dot(att[...], w_ref[...]).astype(BF16)


def kv_grad_kernel(lines, flip_ref, block_ref, later_hbm, row_hbm, *rest):
    col_hbms, dk_ref, dv_ref = rest[:-6], rest[-6], rest[-5]
    row, col, later, sems = rest[-4:]
    copy = pltpu.make_async_copy(later_hbm, later, sems.at[len(col_hbms) + 1])
    copy.start()
    fetch_packed(block_ref, row_hbm, col_hbms, row, col, sems, 1)
    copy.wait()
    low = low_half(dk_ref.shape[0])

    def one(head):
        mine = packed_head(flip_ref, row, col, head)
        if head < row.shape[0]:
            return mine.astype(F32) + later[head ^ flip_ref[0] ^ lines].astype(F32)
        return mine

    for tile in range(row.shape[0]):
        cut = slice(tile * LANES, (tile + 1) * LANES)
        dk, dv = unpaired(one(2 * tile), one(2 * tile + 1), low)
        dk_ref[:, cut] = dk.astype(BF16)
        dv_ref[:, cut] = dv.astype(BF16)


def weight_kernel(*refs):
    count = (len(refs) - 4) // 2
    out_ref, att, grad, sems = refs[2 * count :]
    tokens = att.shape[1] // count
    pairs = []
    for i in range(count):
        at = pl.ds(i * tokens, tokens)
        pairs.append((refs[i], att.at[:, at]))
        pairs.append((refs[count + i], grad.at[at]))
    fetch(pairs, sems)
    out_ref[...] = dot(att[...], grad[...]).astype(BF16).reshape(out_ref.shape)


def plane_sum_kernel(me_ref, in_ref, *rest):
    outs, held = rest[:-1], rest[-1]
    planes = in_ref.shape[0]
    lines, rows, lanes = held.shape
    kept = in_ref.shape[1] // lines
    total = in_ref[0].astype(F32)
    for plane in range(1, planes):
        total = total + in_ref[plane].astype(F32)
    for line in range(lines):
        mine = total[line * kept : (line + 1) * kept]
        cuts = [mine[:, i * lanes : (i + 1) * lanes] for i in range(rows // kept)]
        held[line] = jnp.concatenate(cuts, axis=0)
    for hop, out_ref in enumerate(outs):
        out_ref[...] = held[me_ref[0] ^ hop].astype(BF16)


def line_sum_kernel(factor, *refs):
    total = refs[0][...].astype(F32)
    for ref in refs[1:-1]:
        total = total + ref[...].astype(F32)
    refs[-1][...] = total * factor


def gather_kernel(me_ref, *rest):
    parts, out_ref, held = rest[:-2], rest[-2], rest[-1]
    clips, rows, lanes = held.shape
    kept = out_ref.shape[0] // clips
    for hop, ref in enumerate(parts):
        held[me_ref[0] ^ hop] = ref[...]
    for clip in range(clips):
        for at in range(rows):
            to = (at % kept) * clips + clip
            cut = slice(at // kept * lanes, (at // kept + 1) * lanes)
            out_ref[to : to + 1, cut] = held[clip, at : at + 1]


def swapped(array, axes):
    return lax.all_to_all(array, axes, split_axis=0, concat_axis=0, tiled=True)


def on_device(queries, keys, values, out_grad, w_out):
    _, tokens, width = queries.shape
    row_axes, plane_axes, line_axes = ("yl", "z"), ("b", "yl"), ("d", "z")
    clips, blocks = lax.axis_size("d"), lax.axis_size("b")
    lines = lax.axis_size("z")
    yl = lax.axis_size("yl")
    members = yl * lines
    planes = blocks * yl
    positions = blocks * members
    heads = width // DH // 2
    part = tokens // blocks
    q, k, v, og = (a.reshape(tokens, width) for a in (queries, keys, values, out_grad))
    block_index = lax.axis_index("b").astype(jnp.int32).reshape(1)
    clip_index = lax.axis_index("d").astype(jnp.int32).reshape(1)
    line_index = lax.axis_index("z").astype(jnp.int32).reshape(1)
    flip = (block_index & 1) * lines

    project = 2 * tokens * width * width
    sems = pltpu.SemaphoreType.DMA
    col_piece = shape(2 * part, heads * LANES)
    row_in, *col_in = call(
        pack_kernel,
        (shape(heads, 2 * tokens, LANES), *[col_piece] * blocks),
        (flip, block_index, q, k, v, og, w_out),
        scratch=(
            pltpu.VMEM((tokens, width), BF16),
            pltpu.VMEM(w_out.shape, BF16),
            *[pltpu.VMEM((tokens, width), BF16)] * 5,
            sems((5,)),
        ),
        flops=project,
        vmem=ROOM,
        specs=[SMEM] * 2 + [HBM] * 5,
    )
    row_got = swapped(row_in, row_axes)

    def to_members(pieces):
        got = dict(enumerate(pieces))
        for hop in range(1, blocks):
            got[hop] = lax.ppermute(pieces[hop], "b", [(i, i ^ hop) for i in range(blocks)])
        return [got[hop] for hop in range(blocks)]

    row_got, og_later, *col_got = lax.optimization_barrier((row_got, og, *to_members(col_in)))
    onward = [(i * yl + j, (i + 1) * yl + j ^ 1) for i in range(blocks - 1) for j in range(yl)]
    prev = lax.ppermute(row_got[:, :tokens], ("b", "yl"), onward)
    col_res = call(
        col_kernel,
        (col_piece,) * blocks,
        (block_index, *col_got),
        scratch=(pltpu.VMEM((blocks, 2 * part, heads * LANES), BF16), sems((blocks,))),
        flops=heads * 12 * tokens * tokens * LANES,
        specs=[SMEM] + [HBM] * blocks,
    )
    beside, beyond = (
        lax.ppermute(og_later, "d", [(i, i ^ hop) for i in range(clips)]) for hop in (1, 2)
    )
    col_res = call(
        col_kernel,
        (col_piece,) * blocks,
        (block_index, *col_got),
        scratch=(pltpu.VMEM((blocks, 2 * part, heads * LANES), BF16), sems((blocks,))),
        flops=heads * 12 * tokens * tokens * LANES,
        specs=[SMEM] + [HBM] * blocks,
    )
    other_grads = [
        lax.ppermute(og_later, "d", [(i, i ^ hop) for i in range(clips)])
        for hop in range(1, clips)
    ]
    prev, col_res = lax.optimization_barrier((prev, col_res))
    span = members * tokens
    window = span + tokens
    row_res = call(
        row_kernel,
        shape(members, 3 * tokens, LANES),
        (block_index, row_got, prev),
        scratch=(
            pltpu.VMEM((2 * members, tokens, LANES), BF16),
            pltpu.VMEM((members, tokens, LANES), BF16),
            pltpu.VMEM((LANES, 2 * span), BF16),
            pltpu.VMEM((2 * span, LANES), F32),
            pltpu.VMEM((2, window, tokens), F32),
            pltpu.VMEM((2, window, tokens), F32),
            pltpu.VMEM((2, window, 2 * tokens), BF16),
            sems((3,)),
        ),
        flops=members * 12 * window * tokens * LANES,
        specs=[SMEM, HBM, HBM],
    )
    row_res, col_res, beside, beyond = lax.optimization_barrier(
        (row_res, col_res, beside, beyond)
    )
    row_back = swapped(row_res, row_axes)
    col_back = to_members(col_res)
    other_grads = [
        beside,
        beyond,
        lax.ppermute(beyond, "d", [(i, i ^ 1) for i in range(clips)]),
    ]
    share = width // clips
    piece = share // planes
    kept = piece // lines
    packed = (pltpu.VMEM((heads, tokens, LANES), BF16), pltpu.VMEM((blocks, part, width), BF16))
    turned = call(
        functools.partial(turn_kernel, clips),
        (shape(share, tokens),) * clips,
        (flip, block_index, clip_index, row_back, *col_back),
        scratch=(*packed, pltpu.VMEM((width, tokens), F32), sems((blocks + 1,))),
        specs=[SMEM] * 3 + [HBM] * (blocks + 1),
    )
    att_got = [turned[0]] + [
        lax.ppermute(turned[hop], "d", [(i, i ^ hop) for i in range(clips)])
        for hop in range(1, clips)
    ]
    later = lax.ppermute(
        row_back[:, 2 * tokens :], "b", [(i + 1, i) for i in range(blocks - 1)]
    )
    layer_out, query_grad = call(
        layer_kernel,
        (shape(tokens, width), shape(tokens, width)),
        (flip, block_index, w_out, row_back, *col_back),
        scratch=(
            *packed,
            pltpu.VMEM((tokens, width), BF16),
            pltpu.VMEM(w_out.shape, BF16),
            sems((blocks + 2,)),
        ),
        flops=project,
        specs=[SMEM] * 2 + [HBM] * (blocks + 2),
    )
    key_grad, value_grad = call(
        functools.partial(kv_grad_kernel, lines),
        (shape(tokens, width), shape(tokens, width)),
        (flip, block_index, later, row_back, *col_back),
        scratch=(
            *packed,
            pltpu.VMEM((heads, tokens, LANES), BF16),
            sems((blocks + 2,)),
        ),
        specs=[SMEM] * 2 + [HBM] * (blocks + 2),
    )
    att_got, layer_out = lax.optimization_barrier((att_got, layer_out))
    partial = call(
        weight_kernel,
        shape(planes, piece, width),
        (*att_got, og, *other_grads),
        scratch=(
            pltpu.VMEM((share, clips * tokens), BF16),
            pltpu.VMEM((clips * tokens, width), BF16),
            sems((2 * clips,)),
        ),
        flops=project,
        specs=[HBM] * (2 * clips),
    )
    lanes = kept * width // piece

    def paired_off(pieces, axis, count):
        return [pieces[0]] + [
            lax.ppermute(pieces[hop], axis, [(i, i ^ hop) for i in range(count)])
            for hop in range(1, count)
        ]

    summed = call(
        plane_sum_kernel,
        (shape(piece, lanes),) * lines,
        (line_index, swapped(partial, plane_axes)),
        scratch=(pltpu.VMEM((lines, piece, lanes), F32),),
        specs=[SMEM, VMEM],
    )
    factor = 1.0 / math.sqrt(clips * tokens * positions)
    total = call(
        functools.partial(line_sum_kernel, factor),
        shape(piece, lanes, dtype=F32),
        paired_off(summed, "z", lines),
    )
    weight_grad = call(
        gather_kernel,
        shape(kept * clips, width, dtype=F32),
        (clip_index, *paired_off([total] * clips, "d", clips)),
        scratch=(pltpu.VMEM((clips, piece, lanes), F32),),
        specs=[SMEM] + [VMEM] * clips,
    )
    whole = (1, tokens, width)
    return (
        layer_out.reshape(whole),
        query_grad.reshape(whole),
        key_grad.reshape(whole),
        value_grad.reshape(whole),
        weight_grad,
    )


def solution(mesh):
    clips, positions = mesh.devices.shape
    members = 8
    lines = 4
    split = (clips, positions // members, members // lines, lines)
    inner = Mesh(mesh.devices.reshape(split), ("d", "b", "yl", "z"))
    ctx = ("b", "yl", "z")
    placed = P("d", ctx, None)
    return jax.shard_map(
        on_device,
        mesh=inner,
        in_specs=(placed, placed, placed, placed, P()),
        out_specs=(placed, placed, placed, placed, P(ctx, None)),
        check_vma=False,
    )
```

```python
import functools
import math

import jax
import jax.numpy as jnp
from jax import lax
from jax.experimental import pallas as pl
from jax.experimental.pallas import tpu as pltpu
from jax.sharding import Mesh
from jax.sharding import PartitionSpec as P

DH = 64
STRIDE = 1024
LANES = 128
BF16 = jnp.bfloat16
F32 = jnp.float32
ROOM = 60 << 20
FAR_FIRST = (5, 3, 7, 1, 4, 2, 6, 0)
SCALE = 1.0 / math.sqrt(DH)
SCALE_LOG2 = SCALE / math.log(2.0)
NT = (((1,), (1,)), ((), ()))
NN = (((1,), (0,)), ((), ()))
VMEM = pl.BlockSpec(memory_space=pltpu.VMEM)
SMEM = pl.BlockSpec(memory_space=pltpu.SMEM)
HBM = pl.BlockSpec(memory_space=pltpu.HBM)


def dot(a, b, dims=NN):
    return lax.dot_general(a, b, dims, preferred_element_type=F32)


def call(kernel, out_shape, args, scratch=(), flops=0, vmem=52 << 20, specs=None):
    moved = sum(a.size * a.dtype.itemsize for a in args)
    outs = out_shape if isinstance(out_shape, tuple) else (out_shape,)
    moved += sum(math.prod(o.shape) * o.dtype.itemsize for o in outs)
    return pl.pallas_call(
        kernel,
        out_shape=out_shape,
        in_specs=specs or [VMEM] * len(args),
        out_specs=jax.tree.map(lambda _: VMEM, out_shape),
        scratch_shapes=list(scratch),
        compiler_params=pltpu.CompilerParams(vmem_limit_bytes=vmem),
        cost_estimate=pl.CostEstimate(flops=flops, bytes_accessed=moved, transcendentals=0),
    )(*args)


def shape(*dims, dtype=BF16):
    return jax.ShapeDtypeStruct(dims, dtype)


def low_half(rows):
    return lax.broadcasted_iota(jnp.int32, (rows, LANES), 1) < DH


def swap(tile):
    return pltpu.roll(tile, DH, 1)


def paired(a, b, low):
    a, b = a.astype(F32), b.astype(F32)
    first = jnp.where(low, a, swap(b))
    second = jnp.where(low, swap(a), b)
    return first.astype(BF16), second.astype(BF16)


def fetch(pairs, sems):
    copies = [
        pltpu.make_async_copy(source, target, sems.at[i])
        for i, (source, target) in enumerate(pairs)
    ]
    for copy in copies:
        copy.start()
    for copy in copies:
        copy.wait()


def pack_kernel(
    flip_ref, me_ref, q_hbm, k_hbm, v_hbm, og_hbm, w_hbm, row_ref, *rest
):
    outs = rest[:-8]
    og_ref, w_ref, k_ref, v_ref, q_ref, kv_all, qg_all, sems = rest[-8:]
    tokens, width = og_ref.shape
    half = width // 2
    pairs = ((k_hbm, k_ref), (v_hbm, v_ref), (q_hbm, q_ref), (og_hbm, og_ref), (w_hbm, w_ref))
    copies = [
        pltpu.make_async_copy(source, target, sems.at[i])
        for i, (source, target) in enumerate(pairs)
    ]
    for copy in copies:
        copy.start()
    low = low_half(tokens)
    heads = half // DH

    def put(tile, one, two, rows, both):
        cut = slice(tile * LANES, (tile + 1) * LANES)
        for side, value in enumerate(paired(one[:, cut], two[:, cut], low)):
            head = 2 * tile + side
            if head < heads:
                row_ref[head ^ flip_ref[0], rows] = value
            else:
                both[:, (head - heads) * LANES : (head - heads + 1) * LANES] = value

    for copy in copies[:3]:
        copy.wait()
    for tile in range(width // LANES):
        put(tile, k_ref, v_ref, slice(0, tokens), kv_all)
    for copy in copies[3:]:
        copy.wait()
    og_ref[...] = dot(og_ref[...], w_ref[...], NT).astype(BF16)
    for tile in range(width // LANES):
        put(tile, q_ref, og_ref, slice(tokens, 2 * tokens), qg_all)
    part = tokens // len(outs)
    for slot, out_ref in enumerate(outs):
        rows = pl.ds(pl.multiple_of((me_ref[0] ^ slot) * part, part), part)
        out_ref[:part] = kv_all[rows]
        out_ref[part:] = qg_all[rows]


def split_diag(qg, low, factor=1.0):
    zero = jnp.zeros_like(qg)
    grad = qg * BF16(factor) if factor != 1.0 else qg
    return jnp.concatenate([jnp.where(low, qg, zero), jnp.where(low, zero, grad)], axis=0)


def col_kernel(me_ref, *rest):
    count = (len(rest) - 2) // 2
    sources, outs, held, sems = rest[:count], rest[count : 2 * count], rest[-2], rest[-1]
    fetch([(source, held.at[i]) for i, source in enumerate(sources)], sems)
    blocks, rows, width = held.shape
    part = rows // 2
    tokens = blocks * part
    low = low_half(tokens)
    key = lax.broadcasted_iota(jnp.int32, (tokens, tokens), 0)
    query = lax.broadcasted_iota(jnp.int32, (tokens, tokens), 1)
    flip = me_ref[0] * part
    allowed = ((key ^ flip) <= (query ^ flip)) & (((query ^ key) & (part - 1)) == 0)
    heads = range(width // LANES)
    cuts = [slice(head * LANES, (head + 1) * LANES) for head in heads]
    kvs = [held[:, :part, cut].reshape(tokens, LANES) for cut in cuts]
    qgs = [held[:, part:, cut].reshape(tokens, LANES) for cut in cuts]
    boths = [dot(kv, split_diag(qg, low, SCALE), NT) for kv, qg in zip(kvs, qgs)]
    pairs = []
    for both in boths:
        score = jnp.where(allowed, both[:, :tokens] * SCALE_LOG2, -jnp.inf)
        weight = jnp.exp2(score - jnp.max(score, axis=0, keepdims=True))
        grad = both[:, tokens:]
        scaled = 1.0 / jnp.sum(weight, axis=0, keepdims=True)
        prob = weight * scaled
        delta = jnp.sum(prob * grad, axis=0, keepdims=True)
        score_grad = prob * (grad - delta)
        pairs.append(jnp.concatenate([score_grad.astype(BF16), prob.astype(BF16)], axis=1))
    kv_grads = [dot(pair, split_diag(qg, low)).astype(BF16) for pair, qg in zip(pairs, qgs)]
    flats = [dot(kv.astype(F32).T.astype(BF16), pair) for kv, pair in zip(kvs, pairs)]
    for cut, flat, kv_grad in zip(cuts, flats, kv_grads):
        back = jnp.concatenate([flat[:DH, :tokens], flat[DH:, tokens:]], axis=0)
        back = back.T.astype(BF16)
        for slot, out_ref in enumerate(outs):
            at = slice(slot * part, (slot + 1) * part)
            out_ref[:part, cut] = back[at]
            out_ref[part:, cut] = kv_grad[at]


def row_kernel(first_ref, in_hbm, prev_hbm, out_ref, kv, qg, kv_t, acc, score, grad, pair, sems):
    tiles, size, _ = qg.shape
    span = tiles * size
    chunks = tiles + 1
    low = low_half(size)
    bias = jnp.where(first_ref[0] == 0, -jnp.inf, 0.0).astype(F32)
    fetch(
        (
            (in_hbm.at[:, :size], kv.at[tiles:]),
            (in_hbm.at[:, size:], qg),
            (prev_hbm, kv.at[:tiles]),
        ),
        sems,
    )
    acc[...] = jnp.zeros_like(acc)
    key = lax.broadcasted_iota(jnp.int32, (size, size), 0)
    query = lax.broadcasted_iota(jnp.int32, (size, size), 1)

    def turn(block):
        kv_t[:, block * size : (block + 1) * size] = kv[block].astype(F32).T.astype(BF16)

    def scores(tile):
        slot = tile % 2
        diag = split_diag(qg[tile], low, SCALE)
        top = None
        for chunk in range(chunks):
            rows = slice(chunk * size, (chunk + 1) * size)
            both = dot(kv[tile + chunk], diag, NT)
            now = both[:, :size] * SCALE_LOG2
            if chunk == 0:
                now = jnp.where(key > query, now, -jnp.inf)
            if chunk == chunks - 1:
                now = jnp.where(key <= query, now, -jnp.inf)
            if tile + chunk < tiles:
                now = now + bias
            score[slot, rows] = now
            grad[slot, rows] = both[:, size:]
            best = jnp.max(now, axis=0, keepdims=True)
            top = best if top is None else jnp.maximum(top, best)
        return top

    def softmax(tile, top):
        slot = tile % 2
        total = jnp.zeros((1, size), F32)
        inner = jnp.zeros((1, size), F32)
        for chunk in range(chunks):
            rows = slice(chunk * size, (chunk + 1) * size)
            weight = jnp.exp2(score[slot, rows] - top)
            score[slot, rows] = weight
            total = total + jnp.sum(weight, axis=0, keepdims=True)
            inner = inner + jnp.sum(weight * grad[slot, rows], axis=0, keepdims=True)
        scaled = 1.0 / total
        delta = inner * scaled
        for chunk in range(chunks):
            rows = slice(chunk * size, (chunk + 1) * size)
            prob = score[slot, rows] * scaled
            pair[slot, rows, :size] = (prob * (grad[slot, rows] - delta)).astype(BF16)
            pair[slot, rows, size:] = prob.astype(BF16)

    def products(tile):
        slot = tile % 2
        window = slice(tile * size, (tile + chunks) * size)
        acc[window] += dot(pair[slot], split_diag(qg[tile], low))
        flat = dot(kv_t[:, window], pair[slot])
        back = jnp.concatenate([flat[:DH, :size], flat[DH:, size:]], axis=0)
        out_ref[tile, :size] = back.T.astype(BF16)

    top = scores(0)
    for block in range(chunks):
        turn(block)
    for tile in range(tiles):
        later = scores(tile + 1) if tile + 1 < tiles else None
        softmax(tile, top)
        products(tile)
        if tile + 1 < tiles:
            turn(tile + chunks)
        top = later
    for tile in range(tiles):
        own = acc[span + tile * size : span + (tile + 1) * size]
        out_ref[tile, size : 2 * size] = own.astype(BF16)
        out_ref[tile, 2 * size :] = acc[tile * size : (tile + 1) * size].astype(BF16)


def unpaired(first, second, low):
    first, second = first.astype(F32), second.astype(F32)
    return jnp.where(low, first, swap(second)), jnp.where(low, swap(first), second)


def fetch_packed(block_ref, row_hbm, col_hbms, row, col, sems, which):
    tokens, part = row.shape[1], col.shape[1]
    pairs = [(row_hbm.at[:, which * tokens : (which + 1) * tokens], row)]
    for hop, col_hbm in enumerate(col_hbms):
        source = col_hbm.at[which * part : (which + 1) * part]
        pairs.append((source, col.at[block_ref[0] ^ hop]))
    fetch(pairs, sems)


def packed_head(flip_ref, row, col, head):
    heads, tokens, _ = row.shape
    if head < heads:
        return row[head ^ flip_ref[0]]
    cut = slice((head - heads) * LANES, (head - heads + 1) * LANES)
    return col[:, :, cut].reshape(tokens, LANES)


def turn_kernel(clips, flip_ref, block_ref, me_ref, row_hbm, *rest):
    col_hbms, outs = rest[: -clips - 4], rest[-clips - 4 : -4]
    row, col, turned, sems = rest[-4:]
    fetch_packed(block_ref, row_hbm, col_hbms, row, col, sems, 0)
    share, tokens = outs[0].shape
    low = low_half(tokens)
    for tile in range(row.shape[0]):
        first = packed_head(flip_ref, row, col, 2 * tile).astype(F32)
        second = packed_head(flip_ref, row, col, 2 * tile + 1).astype(F32)
        att = jnp.where(low, swap(first), second)
        turned[tile * LANES : (tile + 1) * LANES] = att.T
    for hop, out_ref in enumerate(outs):
        out_ref[...] = turned[pl.ds(me_ref[0] ^ hop, share, stride=clips)].astype(BF16)


def layer_kernel(flip_ref, block_ref, w_hbm, row_hbm, *rest):
    col_hbms, out_ref, dq_ref = rest[:-7], rest[-7], rest[-6]
    row, col, att, w_ref, sems = rest[-5:]
    copy = pltpu.make_async_copy(w_hbm, w_ref, sems.at[len(col_hbms) + 1])
    copy.start()
    fetch_packed(block_ref, row_hbm, col_hbms, row, col, sems, 0)
    low = low_half(att.shape[0])
    for tile in range(row.shape[0]):
        cut = slice(tile * LANES, (tile + 1) * LANES)
        first = packed_head(flip_ref, row, col, 2 * tile)
        second = packed_head(flip_ref, row, col, 2 * tile + 1)
        dq, out = unpaired(first, second, low)
        dq_ref[:, cut] = dq.astype(BF16)
        att[:, cut] = out.astype(BF16)
    copy.wait()
    out_ref[...] = dot(att[...], w_ref[...]).astype(BF16)


def kv_grad_kernel(lines, flip_ref, block_ref, later_hbm, row_hbm, *rest):
    col_hbms, dk_ref, dv_ref = rest[:-6], rest[-6], rest[-5]
    row, col, later, sems = rest[-4:]
    copy = pltpu.make_async_copy(later_hbm, later, sems.at[len(col_hbms) + 1])
    copy.start()
    fetch_packed(block_ref, row_hbm, col_hbms, row, col, sems, 1)
    copy.wait()
    low = low_half(dk_ref.shape[0])

    def one(head):
        mine = packed_head(flip_ref, row, col, head)
        if head < row.shape[0]:
            return mine.astype(F32) + later[head ^ flip_ref[0] ^ lines].astype(F32)
        return mine

    for tile in range(row.shape[0]):
        cut = slice(tile * LANES, (tile + 1) * LANES)
        dk, dv = unpaired(one(2 * tile), one(2 * tile + 1), low)
        dk_ref[:, cut] = dk.astype(BF16)
        dv_ref[:, cut] = dv.astype(BF16)


def weight_kernel(*refs):
    count = (len(refs) - 4) // 2
    out_ref, att, grad, sems = refs[2 * count :]
    tokens = att.shape[1] // count
    pairs = []
    for i in range(count):
        at = pl.ds(i * tokens, tokens)
        pairs.append((refs[i], att.at[:, at]))
        pairs.append((refs[count + i], grad.at[at]))
    fetch(pairs, sems)
    out_ref[...] = dot(att[...], grad[...]).astype(BF16).reshape(out_ref.shape)


def plane_sum_kernel(me_ref, in_ref, *rest):
    outs, held = rest[:-1], rest[-1]
    planes = in_ref.shape[0]
    lines, rows, lanes = held.shape
    kept = in_ref.shape[1] // lines
    total = in_ref[0].astype(F32)
    for plane in range(1, planes):
        total = total + in_ref[plane].astype(F32)
    for line in range(lines):
        mine = total[line * kept : (line + 1) * kept]
        cuts = [mine[:, i * lanes : (i + 1) * lanes] for i in range(rows // kept)]
        held[line] = jnp.concatenate(cuts, axis=0)
    for hop, out_ref in enumerate(outs):
        out_ref[...] = held[me_ref[0] ^ hop].astype(BF16)


def line_sum_kernel(factor, *refs):
    total = refs[0][...].astype(F32)
    for ref in refs[1:-1]:
        total = total + ref[...].astype(F32)
    refs[-1][...] = total * factor


def gather_kernel(me_ref, *rest):
    parts, out_ref, held = rest[:-2], rest[-2], rest[-1]
    clips, rows, lanes = held.shape
    kept = out_ref.shape[0] // clips
    for hop, ref in enumerate(parts):
        held[me_ref[0] ^ hop] = ref[...]
    for clip in range(clips):
        for at in range(rows):
            to = (at % kept) * clips + clip
            cut = slice(at // kept * lanes, (at // kept + 1) * lanes)
            out_ref[to : to + 1, cut] = held[clip, at : at + 1]


def swapped(array, axes):
    return lax.all_to_all(array, axes, split_axis=0, concat_axis=0, tiled=True)


def on_device(queries, keys, values, out_grad, w_out):
    _, tokens, width = queries.shape
    row_axes, plane_axes, line_axes = ("yl", "z"), ("b", "yl"), ("d", "z")
    clips, blocks = lax.axis_size("d"), lax.axis_size("b")
    lines = lax.axis_size("z")
    yl = lax.axis_size("yl")
    members = yl * lines
    planes = blocks * yl
    positions = blocks * members
    heads = width // DH // 2
    part = tokens // blocks
    q, k, v, og = (a.reshape(tokens, width) for a in (queries, keys, values, out_grad))
    block_index = lax.axis_index("b").astype(jnp.int32).reshape(1)
    clip_index = lax.axis_index("d").astype(jnp.int32).reshape(1)
    line_index = lax.axis_index("z").astype(jnp.int32).reshape(1)
    flip = (block_index & 1) * lines

    project = 2 * tokens * width * width
    sems = pltpu.SemaphoreType.DMA
    col_piece = shape(2 * part, heads * LANES)
    row_in, *col_in = call(
        pack_kernel,
        (shape(heads, 2 * tokens, LANES), *[col_piece] * blocks),
        (flip, block_index, q, k, v, og, w_out),
        scratch=(
            pltpu.VMEM((tokens, width), BF16),
            pltpu.VMEM(w_out.shape, BF16),
            *[pltpu.VMEM((tokens, width), BF16)] * 5,
            sems((5,)),
        ),
        flops=project,
        vmem=ROOM,
        specs=[SMEM] * 2 + [HBM] * 5,
    )
    row_got = swapped(row_in, row_axes)

    def tied(first, second, pieces):
        first, second, *moved = lax.optimization_barrier(
            (first, second, *(pieces[hop] for hop in FAR_FIRST))
        )
        return first, second, [moved[FAR_FIRST.index(hop)] for hop in range(blocks)]

    def to_members(pieces):
        got = dict(enumerate(pieces))
        for hop in range(1, blocks):
            got[hop] = lax.ppermute(pieces[hop], "b", [(i, i ^ hop) for i in range(blocks)])
        return [got[hop] for hop in range(blocks)]

    row_got, og_later, col_got = tied(row_got, og, to_members(col_in))
    onward = [(i * yl + j, (i + 1) * yl + j ^ 1) for i in range(blocks - 1) for j in range(yl)]
    prev = lax.ppermute(row_got[:, :tokens], ("b", "yl"), onward)
    col_res = call(
        col_kernel,
        (col_piece,) * blocks,
        (block_index, *col_got),
        scratch=(pltpu.VMEM((blocks, 2 * part, heads * LANES), BF16), sems((blocks,))),
        flops=heads * 12 * tokens * tokens * LANES,
        specs=[SMEM] + [HBM] * blocks,
    )
    beside, beyond = (
        lax.ppermute(og_later, "d", [(i, i ^ hop) for i in range(clips)]) for hop in (1, 2)
    )
    col_res = call(
        col_kernel,
        (col_piece,) * blocks,
        (block_index, *col_got),
        scratch=(pltpu.VMEM((blocks, 2 * part, heads * LANES), BF16), sems((blocks,))),
        flops=heads * 12 * tokens * tokens * LANES,
        specs=[SMEM] + [HBM] * blocks,
    )
    other_grads = [
        lax.ppermute(og_later, "d", [(i, i ^ hop) for i in range(clips)])
        for hop in range(1, clips)
    ]
    prev, col_res = lax.optimization_barrier((prev, col_res))
    span = members * tokens
    window = span + tokens
    row_res = call(
        row_kernel,
        shape(members, 3 * tokens, LANES),
        (block_index, row_got, prev),
        scratch=(
            pltpu.VMEM((2 * members, tokens, LANES), BF16),
            pltpu.VMEM((members, tokens, LANES), BF16),
            pltpu.VMEM((LANES, 2 * span), BF16),
            pltpu.VMEM((2 * span, LANES), F32),
            pltpu.VMEM((2, window, tokens), F32),
            pltpu.VMEM((2, window, tokens), F32),
            pltpu.VMEM((2, window, 2 * tokens), BF16),
            sems((3,)),
        ),
        flops=members * 12 * window * tokens * LANES,
        specs=[SMEM, HBM, HBM],
    )
    row_res, col_res, beside, beyond = lax.optimization_barrier(
        (row_res, col_res, beside, beyond)
    )
    row_back = swapped(row_res, row_axes)
    row_back, _, col_back = tied(row_back, og, to_members(col_res))
    share = width // clips
    piece = share // planes
    kept = piece // lines
    packed = (pltpu.VMEM((heads, tokens, LANES), BF16), pltpu.VMEM((blocks, part, width), BF16))
    turned = call(
        functools.partial(turn_kernel, clips),
        (shape(share, tokens),) * clips,
        (flip, block_index, clip_index, row_back, *col_back),
        scratch=(*packed, pltpu.VMEM((width, tokens), F32), sems((blocks + 1,))),
        specs=[SMEM] * 3 + [HBM] * (blocks + 1),
    )
    turned, beyond = lax.optimization_barrier((turned, beyond))
    other_grads = [
        beside,
        beyond,
        lax.ppermute(beyond, "d", [(i, i ^ 1) for i in range(clips)]),
    ]
    att_got = [turned[0]] + [
        lax.ppermute(turned[hop], "d", [(i, i ^ hop) for i in range(clips)])
        for hop in range(1, clips)
    ]
    later = lax.ppermute(
        row_back[:, 2 * tokens :], "b", [(i + 1, i) for i in range(blocks - 1)]
    )
    layer_out, query_grad = call(
        layer_kernel,
        (shape(tokens, width), shape(tokens, width)),
        (flip, block_index, w_out, row_back, *col_back),
        scratch=(
            *packed,
            pltpu.VMEM((tokens, width), BF16),
            pltpu.VMEM(w_out.shape, BF16),
            sems((blocks + 2,)),
        ),
        flops=project,
        specs=[SMEM] * 2 + [HBM] * (blocks + 2),
    )
    key_grad, value_grad = call(
        functools.partial(kv_grad_kernel, lines),
        (shape(tokens, width), shape(tokens, width)),
        (flip, block_index, later, row_back, *col_back),
        scratch=(
            *packed,
            pltpu.VMEM((heads, tokens, LANES), BF16),
            sems((blocks + 2,)),
        ),
        specs=[SMEM] * 2 + [HBM] * (blocks + 2),
    )
    att_got, layer_out = lax.optimization_barrier((att_got, layer_out))
    partial = call(
        weight_kernel,
        shape(planes, piece, width),
        tuple(att_got[hop] for hop in (2, 3, 1, 0))
        + tuple((og, *other_grads)[hop] for hop in (2, 3, 1, 0)),
        scratch=(
            pltpu.VMEM((share, clips * tokens), BF16),
            pltpu.VMEM((clips * tokens, width), BF16),
            sems((2 * clips,)),
        ),
        flops=project,
        specs=[HBM] * (2 * clips),
    )
    lanes = kept * width // piece

    def paired_off(pieces, axis, count):
        return [pieces[0]] + [
            lax.ppermute(pieces[hop], axis, [(i, i ^ hop) for i in range(count)])
            for hop in range(1, count)
        ]

    summed = call(
        plane_sum_kernel,
        (shape(piece, lanes),) * lines,
        (line_index, swapped(partial, plane_axes)),
        scratch=(pltpu.VMEM((lines, piece, lanes), F32),),
        specs=[SMEM, VMEM],
    )
    factor = 1.0 / math.sqrt(clips * tokens * positions)
    moved = paired_off(summed, "z", lines)
    total = call(
        functools.partial(line_sum_kernel, factor),
        shape(piece, lanes, dtype=F32),
        (moved[2], moved[1], moved[3], moved[0]),
    )
    weight_grad = call(
        gather_kernel,
        shape(kept * clips, width, dtype=F32),
        (clip_index, *paired_off([total] * clips, "d", clips)),
        scratch=(pltpu.VMEM((clips, piece, lanes), F32),),
        specs=[SMEM] + [VMEM] * clips,
    )
    whole = (1, tokens, width)
    return (
        layer_out.reshape(whole),
        query_grad.reshape(whole),
        key_grad.reshape(whole),
        value_grad.reshape(whole),
        weight_grad,
    )


def solution(mesh):
    clips, positions = mesh.devices.shape
    members = 8
    lines = 4
    split = (clips, positions // members, members // lines, lines)
    inner = Mesh(mesh.devices.reshape(split), ("d", "b", "yl", "z"))
    ctx = ("b", "yl", "z")
    placed = P("d", ctx, None)
    return jax.shard_map(
        on_device,
        mesh=inner,
        in_specs=(placed, placed, placed, placed, P()),
        out_specs=(placed, placed, placed, placed, P(ctx, None)),
        check_vma=False,
    )
```

```python
import functools
import math

import jax
import jax.numpy as jnp
from jax import lax
from jax.experimental import pallas as pl
from jax.experimental.pallas import tpu as pltpu
from jax.sharding import Mesh
from jax.sharding import PartitionSpec as P

DH = 64
STRIDE = 1024
LANES = 128
BF16 = jnp.bfloat16
F32 = jnp.float32
ROOM = 60 << 20
FAR_FIRST = (5, 4, 3, 7, 1, 2, 6, 0)
SCALE = 1.0 / math.sqrt(DH)
SCALE_LOG2 = SCALE / math.log(2.0)
NT = (((1,), (1,)), ((), ()))
NN = (((1,), (0,)), ((), ()))
VMEM = pl.BlockSpec(memory_space=pltpu.VMEM)
SMEM = pl.BlockSpec(memory_space=pltpu.SMEM)
HBM = pl.BlockSpec(memory_space=pltpu.HBM)


def dot(a, b, dims=NN):
    return lax.dot_general(a, b, dims, preferred_element_type=F32)


def call(kernel, out_shape, args, scratch=(), flops=0, vmem=52 << 20, specs=None):
    moved = sum(a.size * a.dtype.itemsize for a in args)
    outs = out_shape if isinstance(out_shape, tuple) else (out_shape,)
    moved += sum(math.prod(o.shape) * o.dtype.itemsize for o in outs)
    return pl.pallas_call(
        kernel,
        out_shape=out_shape,
        in_specs=specs or [VMEM] * len(args),
        out_specs=jax.tree.map(lambda _: VMEM, out_shape),
        scratch_shapes=list(scratch),
        compiler_params=pltpu.CompilerParams(vmem_limit_bytes=vmem),
        cost_estimate=pl.CostEstimate(flops=flops, bytes_accessed=moved, transcendentals=0),
    )(*args)


def shape(*dims, dtype=BF16):
    return jax.ShapeDtypeStruct(dims, dtype)


def low_half(rows):
    return lax.broadcasted_iota(jnp.int32, (rows, LANES), 1) < DH


def swap(tile):
    return pltpu.roll(tile, DH, 1)


def paired(a, b, low):
    a, b = a.astype(F32), b.astype(F32)
    first = jnp.where(low, a, swap(b))
    second = jnp.where(low, swap(a), b)
    return first.astype(BF16), second.astype(BF16)


def fetch(pairs, sems):
    copies = [
        pltpu.make_async_copy(source, target, sems.at[i])
        for i, (source, target) in enumerate(pairs)
    ]
    for copy in copies:
        copy.start()
    for copy in copies:
        copy.wait()


def pack_kernel(
    flip_ref, me_ref, q_hbm, k_hbm, v_hbm, og_hbm, w_hbm, row_ref, *rest
):
    outs = rest[:-8]
    og_ref, w_ref, k_ref, v_ref, q_ref, kv_all, qg_all, sems = rest[-8:]
    tokens, width = og_ref.shape
    half = width // 2
    pairs = ((k_hbm, k_ref), (v_hbm, v_ref), (q_hbm, q_ref), (og_hbm, og_ref), (w_hbm, w_ref))
    copies = [
        pltpu.make_async_copy(source, target, sems.at[i])
        for i, (source, target) in enumerate(pairs)
    ]
    for copy in copies:
        copy.start()
    low = low_half(tokens)
    heads = half // DH

    def put(tile, one, two, rows, both):
        cut = slice(tile * LANES, (tile + 1) * LANES)
        for side, value in enumerate(paired(one[:, cut], two[:, cut], low)):
            head = 2 * tile + side
            if head < heads:
                row_ref[head ^ flip_ref[0], rows] = value
            else:
                both[:, (head - heads) * LANES : (head - heads + 1) * LANES] = value

    for copy in copies[:3]:
        copy.wait()
    for tile in range(width // LANES):
        put(tile, k_ref, v_ref, slice(0, tokens), kv_all)
    for copy in copies[3:]:
        copy.wait()
    og_ref[...] = dot(og_ref[...], w_ref[...], NT).astype(BF16)
    for tile in range(width // LANES):
        put(tile, q_ref, og_ref, slice(tokens, 2 * tokens), qg_all)
    part = tokens // len(outs)
    for slot, out_ref in enumerate(outs):
        rows = pl.ds(pl.multiple_of((me_ref[0] ^ slot) * part, part), part)
        out_ref[:part] = kv_all[rows]
        out_ref[part:] = qg_all[rows]


def split_diag(qg, low, factor=1.0):
    zero = jnp.zeros_like(qg)
    grad = qg * BF16(factor) if factor != 1.0 else qg
    return jnp.concatenate([jnp.where(low, qg, zero), jnp.where(low, zero, grad)], axis=0)


def col_kernel(me_ref, *rest):
    count = (len(rest) - 2) // 2
    sources, outs, held, sems = rest[:count], rest[count : 2 * count], rest[-2], rest[-1]
    fetch([(source, held.at[i]) for i, source in enumerate(sources)], sems)
    blocks, rows, width = held.shape
    part = rows // 2
    tokens = blocks * part
    low = low_half(tokens)
    key = lax.broadcasted_iota(jnp.int32, (tokens, tokens), 0)
    query = lax.broadcasted_iota(jnp.int32, (tokens, tokens), 1)
    flip = me_ref[0] * part
    allowed = ((key ^ flip) <= (query ^ flip)) & (((query ^ key) & (part - 1)) == 0)
    heads = range(width // LANES)
    cuts = [slice(head * LANES, (head + 1) * LANES) for head in heads]
    kvs = [held[:, :part, cut].reshape(tokens, LANES) for cut in cuts]
    qgs = [held[:, part:, cut].reshape(tokens, LANES) for cut in cuts]
    boths = [dot(kv, split_diag(qg, low, SCALE), NT) for kv, qg in zip(kvs, qgs)]
    pairs = []
    for both in boths:
        score = jnp.where(allowed, both[:, :tokens] * SCALE_LOG2, -jnp.inf)
        weight = jnp.exp2(score - jnp.max(score, axis=0, keepdims=True))
        grad = both[:, tokens:]
        scaled = 1.0 / jnp.sum(weight, axis=0, keepdims=True)
        prob = weight * scaled
        delta = jnp.sum(prob * grad, axis=0, keepdims=True)
        score_grad = prob * (grad - delta)
        pairs.append(jnp.concatenate([score_grad.astype(BF16), prob.astype(BF16)], axis=1))
    kv_grads = [dot(pair, split_diag(qg, low)).astype(BF16) for pair, qg in zip(pairs, qgs)]
    flats = [dot(kv.astype(F32).T.astype(BF16), pair) for kv, pair in zip(kvs, pairs)]
    for cut, flat, kv_grad in zip(cuts, flats, kv_grads):
        back = jnp.concatenate([flat[:DH, :tokens], flat[DH:, tokens:]], axis=0)
        back = back.T.astype(BF16)
        for slot, out_ref in enumerate(outs):
            at = slice(slot * part, (slot + 1) * part)
            out_ref[:part, cut] = back[at]
            out_ref[part:, cut] = kv_grad[at]


def row_kernel(first_ref, in_hbm, prev_hbm, out_ref, kv, qg, kv_t, acc, score, grad, pair, sems):
    tiles, size, _ = qg.shape
    span = tiles * size
    chunks = tiles + 1
    low = low_half(size)
    bias = jnp.where(first_ref[0] == 0, -jnp.inf, 0.0).astype(F32)
    fetch(
        (
            (in_hbm.at[:, :size], kv.at[tiles:]),
            (in_hbm.at[:, size:], qg),
            (prev_hbm, kv.at[:tiles]),
        ),
        sems,
    )
    acc[...] = jnp.zeros_like(acc)
    key = lax.broadcasted_iota(jnp.int32, (size, size), 0)
    query = lax.broadcasted_iota(jnp.int32, (size, size), 1)

    def turn(block):
        kv_t[:, block * size : (block + 1) * size] = kv[block].astype(F32).T.astype(BF16)

    def scores(tile):
        slot = tile % 2
        diag = split_diag(qg[tile], low, SCALE)
        top = None
        for chunk in range(chunks):
            rows = slice(chunk * size, (chunk + 1) * size)
            both = dot(kv[tile + chunk], diag, NT)
            now = both[:, :size] * SCALE_LOG2
            if chunk == 0:
                now = jnp.where(key > query, now, -jnp.inf)
            if chunk == chunks - 1:
                now = jnp.where(key <= query, now, -jnp.inf)
            if tile + chunk < tiles:
                now = now + bias
            score[slot, rows] = now
            grad[slot, rows] = both[:, size:]
            best = jnp.max(now, axis=0, keepdims=True)
            top = best if top is None else jnp.maximum(top, best)
        return top

    def softmax(tile, top):
        slot = tile % 2
        total = jnp.zeros((1, size), F32)
        inner = jnp.zeros((1, size), F32)
        for chunk in range(chunks):
            rows = slice(chunk * size, (chunk + 1) * size)
            weight = jnp.exp2(score[slot, rows] - top)
            score[slot, rows] = weight
            total = total + jnp.sum(weight, axis=0, keepdims=True)
            inner = inner + jnp.sum(weight * grad[slot, rows], axis=0, keepdims=True)
        scaled = 1.0 / total
        delta = inner * scaled
        for chunk in range(chunks):
            rows = slice(chunk * size, (chunk + 1) * size)
            prob = score[slot, rows] * scaled
            pair[slot, rows, :size] = (prob * (grad[slot, rows] - delta)).astype(BF16)
            pair[slot, rows, size:] = prob.astype(BF16)

    def products(tile):
        slot = tile % 2
        window = slice(tile * size, (tile + chunks) * size)
        acc[window] += dot(pair[slot], split_diag(qg[tile], low))
        flat = dot(kv_t[:, window], pair[slot])
        back = jnp.concatenate([flat[:DH, :size], flat[DH:, size:]], axis=0)
        out_ref[tile, :size] = back.T.astype(BF16)

    top = scores(0)
    for block in range(chunks):
        turn(block)
    for tile in range(tiles):
        later = scores(tile + 1) if tile + 1 < tiles else None
        softmax(tile, top)
        products(tile)
        if tile + 1 < tiles:
            turn(tile + chunks)
        top = later
    for tile in range(tiles):
        own = acc[span + tile * size : span + (tile + 1) * size]
        out_ref[tile, size : 2 * size] = own.astype(BF16)
        out_ref[tile, 2 * size :] = acc[tile * size : (tile + 1) * size].astype(BF16)


def unpaired(first, second, low):
    first, second = first.astype(F32), second.astype(F32)
    return jnp.where(low, first, swap(second)), jnp.where(low, swap(first), second)


def fetch_packed(block_ref, row_hbm, col_hbms, row, col, sems, which):
    tokens, part = row.shape[1], col.shape[1]
    pairs = [(row_hbm.at[:, which * tokens : (which + 1) * tokens], row)]
    for hop, col_hbm in enumerate(col_hbms):
        source = col_hbm.at[which * part : (which + 1) * part]
        pairs.append((source, col.at[block_ref[0] ^ hop]))
    fetch(pairs, sems)


def packed_head(flip_ref, row, col, head):
    heads, tokens, _ = row.shape
    if head < heads:
        return row[head ^ flip_ref[0]]
    cut = slice((head - heads) * LANES, (head - heads + 1) * LANES)
    return col[:, :, cut].reshape(tokens, LANES)


def turn_kernel(clips, flip_ref, block_ref, me_ref, row_hbm, *rest):
    col_hbms, outs = rest[: -clips - 4], rest[-clips - 4 : -4]
    row, col, turned, sems = rest[-4:]
    fetch_packed(block_ref, row_hbm, col_hbms, row, col, sems, 0)
    share, tokens = outs[0].shape
    low = low_half(tokens)
    for tile in range(row.shape[0]):
        first = packed_head(flip_ref, row, col, 2 * tile).astype(F32)
        second = packed_head(flip_ref, row, col, 2 * tile + 1).astype(F32)
        att = jnp.where(low, swap(first), second)
        turned[tile * LANES : (tile + 1) * LANES] = att.T
    for hop, out_ref in enumerate(outs):
        out_ref[...] = turned[pl.ds(me_ref[0] ^ hop, share, stride=clips)].astype(BF16)


def layer_kernel(flip_ref, block_ref, w_hbm, row_hbm, *rest):
    col_hbms, out_ref, dq_ref = rest[:-7], rest[-7], rest[-6]
    row, col, att, w_ref, sems = rest[-5:]
    copy = pltpu.make_async_copy(w_hbm, w_ref, sems.at[len(col_hbms) + 1])
    copy.start()
    fetch_packed(block_ref, row_hbm, col_hbms, row, col, sems, 0)
    low = low_half(att.shape[0])
    for tile in range(row.shape[0]):
        cut = slice(tile * LANES, (tile + 1) * LANES)
        first = packed_head(flip_ref, row, col, 2 * tile)
        second = packed_head(flip_ref, row, col, 2 * tile + 1)
        dq, out = unpaired(first, second, low)
        dq_ref[:, cut] = dq.astype(BF16)
        att[:, cut] = out.astype(BF16)
    copy.wait()
    out_ref[...] = dot(att[...], w_ref[...]).astype(BF16)


def kv_grad_kernel(lines, flip_ref, block_ref, later_hbm, row_hbm, *rest):
    col_hbms, dk_ref, dv_ref = rest[:-6], rest[-6], rest[-5]
    row, col, later, sems = rest[-4:]
    copy = pltpu.make_async_copy(later_hbm, later, sems.at[len(col_hbms) + 1])
    copy.start()
    fetch_packed(block_ref, row_hbm, col_hbms, row, col, sems, 1)
    copy.wait()
    low = low_half(dk_ref.shape[0])

    def one(head):
        mine = packed_head(flip_ref, row, col, head)
        if head < row.shape[0]:
            return mine.astype(F32) + later[head ^ flip_ref[0] ^ lines].astype(F32)
        return mine

    for tile in range(row.shape[0]):
        cut = slice(tile * LANES, (tile + 1) * LANES)
        dk, dv = unpaired(one(2 * tile), one(2 * tile + 1), low)
        dk_ref[:, cut] = dk.astype(BF16)
        dv_ref[:, cut] = dv.astype(BF16)


def weight_kernel(*refs):
    count = (len(refs) - 4) // 2
    out_ref, att, grad, sems = refs[2 * count :]
    tokens = att.shape[1] // count
    pairs = []
    for i in range(count):
        at = pl.ds(i * tokens, tokens)
        pairs.append((refs[i], att.at[:, at]))
        pairs.append((refs[count + i], grad.at[at]))
    fetch(pairs, sems)
    out_ref[...] = dot(att[...], grad[...]).astype(BF16).reshape(out_ref.shape)


def plane_sum_kernel(me_ref, in_ref, *rest):
    outs, held = rest[:-1], rest[-1]
    planes = in_ref.shape[0]
    lines, rows, lanes = held.shape
    kept = in_ref.shape[1] // lines
    total = in_ref[0].astype(F32)
    for plane in range(1, planes):
        total = total + in_ref[plane].astype(F32)
    for line in range(lines):
        mine = total[line * kept : (line + 1) * kept]
        cuts = [mine[:, i * lanes : (i + 1) * lanes] for i in range(rows // kept)]
        held[line] = jnp.concatenate(cuts, axis=0)
    for hop, out_ref in enumerate(outs):
        out_ref[...] = held[me_ref[0] ^ hop].astype(BF16)


def line_sum_kernel(factor, *refs):
    total = refs[0][...].astype(F32)
    for ref in refs[1:-1]:
        total = total + ref[...].astype(F32)
    refs[-1][...] = total * factor


def gather_kernel(me_ref, *rest):
    parts, out_ref, held = rest[:-2], rest[-2], rest[-1]
    clips, rows, lanes = held.shape
    kept = out_ref.shape[0] // clips
    for hop, ref in enumerate(parts):
        held[me_ref[0] ^ hop] = ref[...]
    for clip in range(clips):
        for at in range(rows):
            to = (at % kept) * clips + clip
            cut = slice(at // kept * lanes, (at // kept + 1) * lanes)
            out_ref[to : to + 1, cut] = held[clip, at : at + 1]


def swapped(array, axes):
    return lax.all_to_all(array, axes, split_axis=0, concat_axis=0, tiled=True)


def on_device(queries, keys, values, out_grad, w_out):
    _, tokens, width = queries.shape
    row_axes, plane_axes, line_axes = ("yl", "z"), ("b", "yl"), ("d", "z")
    clips, blocks = lax.axis_size("d"), lax.axis_size("b")
    lines = lax.axis_size("z")
    yl = lax.axis_size("yl")
    members = yl * lines
    planes = blocks * yl
    positions = blocks * members
    heads = width // DH // 2
    part = tokens // blocks
    q, k, v, og = (a.reshape(tokens, width) for a in (queries, keys, values, out_grad))
    block_index = lax.axis_index("b").astype(jnp.int32).reshape(1)
    clip_index = lax.axis_index("d").astype(jnp.int32).reshape(1)
    line_index = lax.axis_index("z").astype(jnp.int32).reshape(1)
    flip = (block_index & 1) * lines

    project = 2 * tokens * width * width
    sems = pltpu.SemaphoreType.DMA
    col_piece = shape(2 * part, heads * LANES)
    row_in, *col_in = call(
        pack_kernel,
        (shape(heads, 2 * tokens, LANES), *[col_piece] * blocks),
        (flip, block_index, q, k, v, og, w_out),
        scratch=(
            pltpu.VMEM((tokens, width), BF16),
            pltpu.VMEM(w_out.shape, BF16),
            *[pltpu.VMEM((tokens, width), BF16)] * 5,
            sems((5,)),
        ),
        flops=project,
        vmem=ROOM,
        specs=[SMEM] * 2 + [HBM] * 5,
    )
    row_got = swapped(row_in, row_axes)

    def tied(first, second, pieces):
        first, second, *moved = lax.optimization_barrier(
            (first, second, *(pieces[hop] for hop in FAR_FIRST))
        )
        return first, second, [moved[FAR_FIRST.index(hop)] for hop in range(blocks)]

    def to_members(pieces):
        got = dict(enumerate(pieces))
        for hop in range(1, blocks):
            got[hop] = lax.ppermute(pieces[hop], "b", [(i, i ^ hop) for i in range(blocks)])
        return [got[hop] for hop in range(blocks)]

    row_got, og_later, col_got = tied(row_got, og, to_members(col_in))
    onward = [(i * yl + j, (i + 1) * yl + j ^ 1) for i in range(blocks - 1) for j in range(yl)]
    prev = lax.ppermute(row_got[:, :tokens], ("b", "yl"), onward)
    col_res = call(
        col_kernel,
        (col_piece,) * blocks,
        (block_index, *col_got),
        scratch=(pltpu.VMEM((blocks, 2 * part, heads * LANES), BF16), sems((blocks,))),
        flops=heads * 12 * tokens * tokens * LANES,
        specs=[SMEM] + [HBM] * blocks,
    )
    beside, beyond = (
        lax.ppermute(og_later, "d", [(i, i ^ hop) for i in range(clips)]) for hop in (1, 2)
    )
    col_res = call(
        col_kernel,
        (col_piece,) * blocks,
        (block_index, *col_got),
        scratch=(pltpu.VMEM((blocks, 2 * part, heads * LANES), BF16), sems((blocks,))),
        flops=heads * 12 * tokens * tokens * LANES,
        specs=[SMEM] + [HBM] * blocks,
    )
    other_grads = [
        lax.ppermute(og_later, "d", [(i, i ^ hop) for i in range(clips)])
        for hop in range(1, clips)
    ]
    prev, col_res = lax.optimization_barrier((prev, col_res))
    span = members * tokens
    window = span + tokens
    row_res = call(
        row_kernel,
        shape(members, 3 * tokens, LANES),
        (block_index, row_got, prev),
        scratch=(
            pltpu.VMEM((2 * members, tokens, LANES), BF16),
            pltpu.VMEM((members, tokens, LANES), BF16),
            pltpu.VMEM((LANES, 2 * span), BF16),
            pltpu.VMEM((2 * span, LANES), F32),
            pltpu.VMEM((2, window, tokens), F32),
            pltpu.VMEM((2, window, tokens), F32),
            pltpu.VMEM((2, window, 2 * tokens), BF16),
            sems((3,)),
        ),
        flops=members * 12 * window * tokens * LANES,
        vmem=24 << 20,
        specs=[SMEM, HBM, HBM],
    )
    row_res, col_res, beside, beyond = lax.optimization_barrier(
        (row_res, col_res, beside, beyond)
    )
    row_back = swapped(row_res, row_axes)
    row_back, _, col_back = tied(row_back, og, to_members(col_res))
    share = width // clips
    piece = share // planes
    kept = piece // lines
    packed = (pltpu.VMEM((heads, tokens, LANES), BF16), pltpu.VMEM((blocks, part, width), BF16))
    turned = call(
        functools.partial(turn_kernel, clips),
        (shape(share, tokens),) * clips,
        (flip, block_index, clip_index, row_back, *col_back),
        scratch=(*packed, pltpu.VMEM((width, tokens), F32), sems((blocks + 1,))),
        specs=[SMEM] * 3 + [HBM] * (blocks + 1),
    )
    turned, beyond = lax.optimization_barrier((turned, beyond))
    other_grads = [
        beside,
        beyond,
        lax.ppermute(beyond, "d", [(i, i ^ 1) for i in range(clips)]),
    ]
    att_got = [turned[0]] + [
        lax.ppermute(turned[hop], "d", [(i, i ^ hop) for i in range(clips)])
        for hop in range(1, clips)
    ]
    later = lax.ppermute(
        row_back[:, 2 * tokens :], "b", [(i + 1, i) for i in range(blocks - 1)]
    )
    layer_out, query_grad = call(
        layer_kernel,
        (shape(tokens, width), shape(tokens, width)),
        (flip, block_index, w_out, row_back, *col_back),
        scratch=(
            *packed,
            pltpu.VMEM((tokens, width), BF16),
            pltpu.VMEM(w_out.shape, BF16),
            sems((blocks + 2,)),
        ),
        flops=project,
        specs=[SMEM] * 2 + [HBM] * (blocks + 2),
    )
    key_grad, value_grad = call(
        functools.partial(kv_grad_kernel, lines),
        (shape(tokens, width), shape(tokens, width)),
        (flip, block_index, later, row_back, *col_back),
        scratch=(
            *packed,
            pltpu.VMEM((heads, tokens, LANES), BF16),
            sems((blocks + 2,)),
        ),
        specs=[SMEM] * 2 + [HBM] * (blocks + 2),
    )
    att_got, layer_out = lax.optimization_barrier((att_got, layer_out))
    partial = call(
        weight_kernel,
        shape(planes, piece, width),
        tuple(att_got[hop] for hop in (2, 3, 1, 0))
        + tuple((og, *other_grads)[hop] for hop in (2, 3, 1, 0)),
        scratch=(
            pltpu.VMEM((share, clips * tokens), BF16),
            pltpu.VMEM((clips * tokens, width), BF16),
            sems((2 * clips,)),
        ),
        flops=project,
        specs=[HBM] * (2 * clips),
    )
    lanes = kept * width // piece

    def paired_off(pieces, axis, count):
        return [pieces[0]] + [
            lax.ppermute(pieces[hop], axis, [(i, i ^ hop) for i in range(count)])
            for hop in range(1, count)
        ]

    summed = call(
        plane_sum_kernel,
        (shape(piece, lanes),) * lines,
        (line_index, swapped(partial, plane_axes)),
        scratch=(pltpu.VMEM((lines, piece, lanes), F32),),
        specs=[SMEM, VMEM],
    )
    factor = 1.0 / math.sqrt(clips * tokens * positions)
    moved = paired_off(summed, "z", lines)
    total = call(
        functools.partial(line_sum_kernel, factor),
        shape(piece, lanes, dtype=F32),
        (moved[2], moved[1], moved[3], moved[0]),
    )
    weight_grad = call(
        gather_kernel,
        shape(kept * clips, width, dtype=F32),
        (clip_index, *paired_off([total] * clips, "d", clips)),
        scratch=(pltpu.VMEM((clips, piece, lanes), F32),),
        specs=[SMEM] + [VMEM] * clips,
    )
    whole = (1, tokens, width)
    return (
        layer_out.reshape(whole),
        query_grad.reshape(whole),
        key_grad.reshape(whole),
        value_grad.reshape(whole),
        weight_grad,
    )


def solution(mesh):
    clips, positions = mesh.devices.shape
    members = 8
    lines = 4
    split = (clips, positions // members, members // lines, lines)
    inner = Mesh(mesh.devices.reshape(split), ("d", "b", "yl", "z"))
    ctx = ("b", "yl", "z")
    placed = P("d", ctx, None)
    return jax.shard_map(
        on_device,
        mesh=inner,
        in_specs=(placed, placed, placed, placed, P()),
        out_specs=(placed, placed, placed, placed, P(ctx, None)),
        check_vma=False,
    )
```
